32 devices in a mesh: tm: 4 (over y, x), cells: 8 (over z, core).
Axes of the slice: x: 2, y: 2, z: 4, core: 2. Of those that a mesh axis runs over, the one named last changes fastest.
Arguments:
- footprint: float32 [4, 4, 768, 8192], P('tm', None, None, 'cells'), may hold values from -0.03125 to 0.03125
- flux: float32 [4, 8192, 2048], P('tm', 'cells'), may hold values from -6 to 6
- obs_weight: float32 [4, 768], P('tm'), may hold values from 0.2 to 5
- obs_count: int32 [4], P('tm'), may hold values from 1 to 768, 2304 in all
Outputs:
- normal_image: float32 [4, 8192, 2048], P('tm', 'cells')
The draws below stay inside these ranges and needn't reach their ends.
Inputs may be any that keep to these rules, and one draw needn't show every extreme that they name: `obs_count`: each block has at least one valid slot; one block has all 768 slots valid.
All inputs are finite; a program needn't handle non-finite values.
Results may differ from the reference program's by a relative error of at most 0.0001.
Values sent between devices are 32-bit elements; how exact they have to be, the bound alone decides.
No kernel may reach another device: no remote copies, remote signals or barrier semaphores. Data moves between devices by JAX's collectives and lax.ppermute only.
A program may use at most 128 MiB of HBM per device.

```python
import math
import jax
import jax.numpy as jnp
import numpy as np
from jax import lax

NC = 8192
NOBS = 768
LAGS = 4
K = 2048
NT = 4


def level_of(key, extent, split, least, high):
    level, own = 1.0, jax.random.fold_in(key, 6)
    for dim, parts in split:
        steps = jnp.exp(jax.random.uniform(jax.random.fold_in(own, dim), (parts,), jnp.float32, least / len(split), high / len(split)))
        level = level * jnp.repeat(steps, extent[dim] // parts).reshape([-1 if axis == dim else 1 for axis in range(len(extent))])
    return level


def profile(number_of, total, limit, skew):
    portions = [(1 << 20) // math.isqrt(rank ** skew) + 1 for rank in range(2, number_of + 1)]
    spare, counts = total - limit - (number_of - 1), [1] * (number_of - 1)
    while spare > 0:
        movable = [i for i in range(number_of - 1) if counts[i] < limit]
        whole, remaining = sum([portions[i] for i in movable]), spare
        for i in movable:
            extra = min(limit - counts[i], max(1, remaining * portions[i] // whole), spare)
            counts[i] = counts[i] + extra
            spare = spare - extra
    return np.array([limit] + counts)


def uneven(rng, amount, total, most, lean):
    if amount == 2:
        one = jax.random.randint(rng, (), max(1, total - most), min(most, total - 1) + 1)
        return jnp.stack([one, total - one])
    lengths = jnp.asarray(profile(amount, total, most, lean), jnp.int32)
    pairs = (amount - 1) // 2
    source_of, taker = lengths[1:1 + 2 * pairs:2], lengths[2:2 + 2 * pairs:2]
    margin = jnp.minimum(source_of - 1, most - taker)
    moved = jax.random.randint(jax.random.fold_in(rng, 1), (pairs,), 0, 1 << 20) % (margin + 1)
    lengths = lengths.at[1:1 + 2 * pairs:2].set(source_of - moved).at[2:2 + 2 * pairs:2].set(taker + moved)
    return lengths[jax.random.permutation(jax.random.fold_in(rng, 2), amount)]


def noise(rng, extent, scale, bound, shards=(), held_as=jnp.bfloat16):
    loudness = level_of(rng, extent, shards, -0.22, 0.18) if shards else 1.0
    drawn = jax.random.normal(rng, extent, jnp.float32) * scale * loudness
    return jnp.minimum(jnp.maximum(drawn, -bound), bound).astype(held_as)


def setup_inputs(seed: int = 0) -> dict:
    keys = jax.random.split(jax.random.key(seed), 5)
    footprint = noise(keys[0], (NT, LAGS, NOBS, NC), (LAGS * NC) ** -0.5, 0.03125, ((0, 4), (3, 8)), jnp.float32)
    flux = noise(keys[1], (NT, NC, K), 1.0, 6.0, ((0, 4), (1, 8)), jnp.float32)
    obs_weight = jnp.clip(jnp.exp(math.log(5.0) - 3.218876 * jax.random.uniform(keys[2], (NT, NOBS), jnp.float32) ** level_of(keys[2], (NT, NOBS), ((0, 4),), -0.2, 0.2)), 0.2, 5.0)
    obs_count = uneven(keys[3], NT, NT * NOBS * 3 // 4, NOBS, 0).astype(jnp.int32)
    return {"footprint": footprint, "flux": flux, "obs_weight": obs_weight, "obs_count": obs_count}


def reference(footprint, flux, obs_weight, obs_count):
    highest = lax.Precision.HIGHEST
    block_count = footprint.shape[0]
    lag_count = footprint.shape[1]
    slot_count = footprint.shape[2]
    valid = (jnp.arange(slot_count, dtype=jnp.int32)[None, :] < obs_count[:, None]).astype(jnp.float32)
    row_scale = valid * obs_weight
    weighted_list = []
    for tblock in range(block_count):
        modelled = jnp.zeros((slot_count, flux.shape[2]), jnp.float32)
        for lag_step in range(lag_count):
            if tblock - lag_step >= 0:
                modelled = modelled + jnp.dot(footprint[tblock, lag_step], flux[tblock - lag_step], precision=highest, preferred_element_type=jnp.float32)
        weighted_list.append(row_scale[tblock][:, None] * modelled)
    images = []
    for source in range(block_count):
        image = jnp.zeros((flux.shape[1], flux.shape[2]), jnp.float32)
        for lag_step in range(lag_count):
            if source + lag_step < block_count:
                image = image + lax.dot_general(footprint[source + lag_step, lag_step], weighted_list[source + lag_step], (((0,), (0,)), ((), ())), precision=highest, preferred_element_type=jnp.float32)
        images.append(image)
    return jnp.stack(images)
```

```python
import jax
import jax.numpy as jnp
from jax import lax
from jax.sharding import Mesh, PartitionSpec as P

CHUNKS = 2


def shifted(value, by):
    devices = lax.axis_size("tm")
    pairs = [(i, i + by) for i in range(devices) if 0 <= i + by < devices]
    return lax.ppermute(value, "tm", pairs)


def swapped(value):
    return lax.ppermute(value, "core", [(0, 1), (1, 0)])


def product(left, right):
    return jnp.dot(
        left, right, precision=lax.Precision.HIGH, preferred_element_type=jnp.float32
    )


def adjoint(left, right):
    return lax.dot_general(
        left,
        right,
        (((0,), (0,)), ((), ())),
        precision=lax.Precision.HIGH,
        preferred_element_type=jnp.float32,
    )


def on_device(footprint, flux, obs_weight, obs_count):
    foot = footprint[0]
    lags, slots, _ = foot.shape
    half = flux.shape[2] // 2
    width = half // CHUNKS
    core = lax.axis_index("core")
    valid = (jnp.arange(slots, dtype=jnp.int32) < obs_count[0]).astype(jnp.float32)
    row_scale = valid * obs_weight[0]

    foot_own = [foot[0]] + [shifted(foot[lag], -lag) for lag in range(1, lags)]
    flux_own = lax.dynamic_slice_in_dim(flux[0], core * half, half, 1)
    flux_other = swapped(lax.dynamic_slice_in_dim(flux[0], (1 - core) * half, half, 1))
    foot_other = [swapped(value) for value in foot_own]

    def forward(lag, start, size):
        return product(foot_own[lag], flux_own[:, start:start + size]) + product(
            foot_other[lag], flux_other[:, start:start + size]
        )

    early = forward(0, 0, half)
    for lag in range(1, lags - 1):
        early = early + shifted(forward(lag, 0, half), lag)

    own_parts, other_parts = [], []
    for chunk in range(CHUNKS):
        start = chunk * width
        last = shifted(forward(lags - 1, start, width), lags - 1)
        if chunk:
            last, modelled = lax.optimization_barrier((last, modelled))
        partial = early[:, start:start + width] + last
        modelled = lax.psum(partial, "z")
        scale, arrived = lax.optimization_barrier((row_scale, modelled))
        weighted = scale[:, None] * arrived
        own, other = None, None
        for lag in range(lags):
            here = weighted if lag == 0 else shifted(weighted, -lag)
            term_own, term_other = adjoint(foot_own[lag], here), adjoint(foot_other[lag], here)
            own = term_own if own is None else own + term_own
            other = term_other if other is None else other + term_other
        own_parts.append(own)
        other_parts.append(swapped(other))
    own = jnp.concatenate(own_parts, axis=1)
    other = jnp.concatenate(other_parts, axis=1)
    first = jnp.where(core == 0, own, other)
    second = jnp.where(core == 0, other, own)
    return jnp.concatenate([first, second], axis=1)[None]


def solution(mesh):
    devices = mesh.devices
    split = Mesh(devices.reshape(devices.shape[0], devices.shape[1] // 2, 2), ("tm", "z", "core"))
    cells = ("z", "core")
    placed = (P("tm", None, None, cells), P("tm", cells, None), P("tm", None), P("tm"))
    return jax.shard_map(
        on_device, mesh=split, in_specs=placed, out_specs=P("tm", cells, None), check_vma=False
    )
```

```python
import functools

import jax
import jax.numpy as jnp
from jax import lax
from jax.experimental import pallas as pl
from jax.experimental.pallas import tpu as pltpu
from jax.sharding import Mesh, PartitionSpec as P

CHUNKS = 3
TILE = 256
VMEM_LIMIT = 60 * 1024 * 1024


def shifted(value, by):
    devices = lax.axis_size("tm")
    pairs = [(i, i + by) for i in range(devices) if 0 <= i + by < devices]
    return lax.ppermute(value, "tm", pairs)


def swapped(value):
    return lax.ppermute(value, "core", [(0, 1), (1, 0)])


def together(first, second):
    return lax.optimization_barrier((first, second))


def halves(value):
    high = value.astype(jnp.bfloat16)
    low = (value - high.astype(jnp.float32)).astype(jnp.bfloat16)
    return high, low


def times(left, right, dims):
    return lax.dot_general(left, right, (dims, ((), ())), preferred_element_type=jnp.float32)


def forward_kernel(count, core_ref, *refs):
    foot_own, foot_other = refs[:count], refs[count:2 * count]
    flux_own, flux_other = refs[2 * count:2 * count + 2]
    outs = refs[2 * count + 2:3 * count + 2]
    high_ref, low_ref = refs[3 * count + 2:]
    rows, cells = foot_own[0].shape[-2:]

    @pl.when(pl.program_id(0) == 0)
    def _():
        for i in range(count):
            for side, source in ((0, foot_own[i]), (1, foot_other[i])):
                high, low = halves(source[...].reshape(rows, cells))
                at = (pl.ds(i * rows, rows), pl.ds(side * cells, cells))
                high_ref[at] = high
                low_ref[at] = low

    total = None
    for side, source in ((0, flux_own), (1, flux_other)):
        high, low = halves(source[...].reshape(cells, -1))
        at = pl.ds(side * cells, cells)
        dims = ((1,), (0,))
        term = times(high_ref[:, at], high, dims)
        term = term + times(low_ref[:, at], high, dims)
        term = term + times(high_ref[:, at], low, dims)
        total = term if total is None else total + term
    for i in range(count):
        outs[i][...] = total[i * rows:(i + 1) * rows]


def forward(
    foot_own, own_specs, foot_other, other_specs, rows, flux, flux_other, cells, half, core
):
    count = len(foot_own)
    tile = min(TILE, half)
    steps = half // tile
    work = 2 * count * rows * 2 * cells * half
    outs = pl.pallas_call(
        functools.partial(forward_kernel, count),
        grid_spec=pltpu.PrefetchScalarGridSpec(
            num_scalar_prefetch=1,
            grid=(steps,),
            in_specs=[
                *own_specs,
                *other_specs,
                pl.BlockSpec((1, cells, tile), lambda j, c: (0, 0, c[0] * steps + j)),
                pl.BlockSpec((cells, tile), lambda j, c: (0, j)),
            ],
            out_specs=[pl.BlockSpec((rows, tile), lambda j, c: (0, j))] * count,
            scratch_shapes=[pltpu.VMEM((count * rows, 2 * cells), jnp.bfloat16)] * 2,
        ),
        out_shape=[jax.ShapeDtypeStruct((rows, half), jnp.float32)] * count,
        compiler_params=pltpu.CompilerParams(vmem_limit_bytes=VMEM_LIMIT),
        cost_estimate=pl.CostEstimate(
            flops=3 * work,
            bytes_accessed=4 * (count * rows * (2 * cells + half) + 2 * cells * half),
            transcendentals=0,
        ),
    )(core, *foot_own, *foot_other, flux, flux_other)
    return list(outs)


def adjoint_kernel(count, first, core_ref, *refs):
    foot, weighted = refs[:count], refs[count:2 * count]
    rest = refs[2 * count:]
    before = None if first else rest[0]
    out_ref, high_ref, low_ref = rest[-3:]
    rows, tile = foot[0].shape[-2:]

    @pl.when(pl.program_id(0) == 0)
    def _():
        for i in range(count):
            high, low = halves(weighted[i][...])
            high_ref[pl.ds(i * rows, rows), :] = high
            low_ref[pl.ds(i * rows, rows), :] = low

    slab = jnp.concatenate([foot[i][...].reshape(rows, tile) for i in range(count)], axis=0)
    high, low = halves(slab)
    dims = ((0,), (0,))
    total = times(high, high_ref[...], dims)
    total = total + times(low, high_ref[...], dims)
    total = total + times(high, low_ref[...], dims)
    if not first:
        total = total + before[...]
    out_ref[...] = total


def adjoint(foot, foot_specs, weighted, before, out_shape, at_core, core, cells):
    count = len(foot)
    rows, half = weighted[0].shape
    tile = min(TILE, cells)
    out_spec = pl.BlockSpec((tile, half), lambda j, c: (j, c[0] if at_core else 0))
    first = before is None
    return pl.pallas_call(
        functools.partial(adjoint_kernel, count, first),
        grid_spec=pltpu.PrefetchScalarGridSpec(
            num_scalar_prefetch=1,
            grid=(cells // tile,),
            in_specs=[
                *[spec(tile) for spec in foot_specs],
                *[pl.BlockSpec((rows, half), lambda j, c: (0, 0))] * count,
                *([] if first else [out_spec]),
            ],
            out_specs=out_spec,
            scratch_shapes=[pltpu.VMEM((count * rows, half), jnp.bfloat16)] * 2,
        ),
        out_shape=jax.ShapeDtypeStruct(out_shape, jnp.float32),
        input_output_aliases={} if first else {1 + 2 * count: 0},
        compiler_params=pltpu.CompilerParams(vmem_limit_bytes=VMEM_LIMIT),
        cost_estimate=pl.CostEstimate(
            flops=3 * 2 * count * rows * cells * half,
            bytes_accessed=4 * (count * rows * (cells + half) + 2 * cells * half),
            transcendentals=0,
        ),
    )(core, *foot, *weighted, *([] if first else [before]))


def combine_kernel(scale, same, *refs):
    total = same[...]
    for ref in refs[:-1]:
        total = total + ref[...]
    refs[-1][...] = scale[...] * total


def combine(scale, same, gathered, r):
    rows, half = gathered[0].shape
    tile = min(TILE, half)
    block = pl.BlockSpec((rows, tile), lambda j: (0, j))
    return pl.pallas_call(
        combine_kernel,
        grid=(half // tile,),
        in_specs=[
            pl.BlockSpec((rows, 1), lambda j: (r, 0)),
            block,
            *[block] * len(gathered),
        ],
        out_specs=block,
        out_shape=jax.ShapeDtypeStruct((rows, half), jnp.float32),
        cost_estimate=pl.CostEstimate(
            flops=(len(gathered) + 1) * rows * half,
            bytes_accessed=4 * (len(gathered) + 2) * rows * half,
            transcendentals=0,
        ),
    )(scale, same, *gathered)


def paste_kernel(core_ref, arrived, before, out_ref):
    out_ref[...] = arrived[...]


def paste(arrived, whole, core):
    cells, half = arrived.shape
    tile = min(TILE, cells)
    return pl.pallas_call(
        paste_kernel,
        grid_spec=pltpu.PrefetchScalarGridSpec(
            num_scalar_prefetch=1,
            grid=(cells // tile,),
            in_specs=[
                pl.BlockSpec((tile, half), lambda j, c: (j, 0)),
                pl.BlockSpec(memory_space=pl.ANY),
            ],
            out_specs=pl.BlockSpec((tile, half), lambda j, c: (j, 1 - c[0])),
        ),
        out_shape=jax.ShapeDtypeStruct(whole.shape, jnp.float32),
        input_output_aliases={2: 0},
        cost_estimate=pl.CostEstimate(
            flops=0, bytes_accessed=8 * cells * half, transcendentals=0
        ),
    )(core, arrived, whole)


def on_device(footprint, flux, obs_weight, obs_count):
    _, lags, slots, cells = footprint.shape
    half = flux.shape[2] // 2
    rows = slots // CHUNKS
    core_at = lax.axis_index("core")
    core = core_at.astype(jnp.int32)[None]
    valid = (jnp.arange(slots, dtype=jnp.int32) < obs_count[0]).astype(jnp.float32)
    row_scale = (valid * obs_weight[0])[:, None]
    later = range(1, lags)

    def whole(block):
        return pl.BlockSpec((rows, cells), lambda j, c: (block, 0))

    def column(block):
        return lambda tile: pl.BlockSpec((rows, tile), lambda j, c: (block, j))

    own = [[shifted(footprint[0, lag, :rows], -lag) for lag in later]]
    flux_sent = lax.dynamic_slice_in_dim(flux[0], (1 - core_at) * half, half, 1)
    if half == cells and cells % rows == 0:
        flux_other = foot_other = swapped(jnp.concatenate([flux_sent, footprint[0, 0]], axis=0))
        foot_at = cells // rows
    else:
        flux_other, foot_other = swapped(flux_sent), swapped(footprint[0, 0])
        foot_at = 0
    chunks = range(CHUNKS)
    same = forward(
        [footprint] * CHUNKS,
        [pl.BlockSpec((1, 1, rows, cells), lambda j, c, r=r: (0, 0, r, 0)) for r in chunks],
        [foot_other] * CHUNKS,
        [whole(foot_at + r) for r in chunks],
        rows, flux, flux_other, cells, half, core,
    )
    own_specs = [whole(0)] * len(later)
    other_specs = [whole(i) for i in range(len(later))]

    partial, other, weighted = [], [], []
    for r in chunks:
        if r > 0:
            pieces = []
            for lag in later:
                piece = footprint[0, lag, r * rows:(r + 1) * rows]
                if r == 1:
                    piece, same[0] = together(piece, same[0])
                else:
                    piece, gathered[lag - 1] = together(piece, gathered[lag - 1])
                pieces.append(shifted(piece, -lag))
            own.append(pieces)
            if r > 1:
                own[r][0], weighted[r - 2] = together(own[r][0], weighted[r - 2])
            gathered = [shifted(terms[lag - 1], lag) for lag in later]
            for i in range(len(later)):
                own[r][i], gathered[i] = together(own[r][i], gathered[i])
            partial.append(combine(row_scale, same[r - 1], gathered, r - 1))
            own[r][0], partial[r - 1] = together(own[r][0], partial[r - 1])
            if r > 1:
                partial[r - 1], weighted[r - 2] = together(partial[r - 1], weighted[r - 2])
            weighted.append(lax.psum(partial[r - 1], "z"))
        else:
            own[r][0], same[0] = together(own[r][0], same[0])
        other.append(swapped(jnp.concatenate(own[r], axis=0)))
        terms = forward(
            own[r], own_specs, [other[r]] * len(later), other_specs,
            rows, flux, flux_other, cells, half, core,
        )
    gathered = [shifted(terms[lag - 1], lag) for lag in later]
    partial.append(combine(row_scale, same[r], gathered, r))
    partial[r], weighted[r - 1] = together(partial[r], weighted[r - 1])
    weighted.append(lax.psum(partial[r], "z"))

    sent = []
    for r in chunks:
        if r > 0:
            for i in range(len(later)):
                weighted[r], sent[r - 1][i] = together(weighted[r], sent[r - 1][i])
        sent.append([shifted(weighted[r], -lag) for lag in later])
    mine, theirs = None, None
    for r in chunks:
        here = [weighted[r], *sent[r]]
        if r + 1 < CHUNKS:
            here[0], _ = together(here[0], weighted[r + 1])

        def own_rows(tile, r=r):
            return pl.BlockSpec((1, 1, rows, tile), lambda j, c: (0, 0, r, j))

        theirs = adjoint(
            [foot_other] + [other[r]] * len(later),
            [column(foot_at + r)] + [column(i) for i in range(len(later))],
            here, theirs, (cells, half), False, core, cells,
        )
        mine = adjoint(
            [footprint, *own[r]], [own_rows] + [column(0)] * len(later),
            here, mine, (cells, 2 * half), True, core, cells,
        )
    return paste(swapped(theirs), mine, core)[None]


def solution(mesh):
    devices = mesh.devices
    split = Mesh(devices.reshape(devices.shape[0], devices.shape[1] // 2, 2), ("tm", "z", "core"))
    cells = ("z", "core")
    placed = (P("tm", None, None, cells), P("tm", cells, None), P("tm", None), P("tm"))
    return jax.shard_map(
        on_device, mesh=split, in_specs=placed, out_specs=P("tm", cells, None), check_vma=False
    )
```

```python
import functools

import jax
import jax.numpy as jnp
from jax import lax
from jax.experimental import pallas as pl
from jax.experimental.pallas import tpu as pltpu
from jax.sharding import Mesh, PartitionSpec as P

CHUNKS = 4
TILE = 256
WIDE = 512
LIGHT = pl.CostEstimate(flops=1, bytes_accessed=1, transcendentals=0)
VMEM_LIMIT = 60 * 1024 * 1024


def shifted(value, by):
    devices = lax.axis_size("tm")
    pairs = [(i, i + by) for i in range(devices) if 0 <= i + by < devices]
    return lax.ppermute(value, "tm", pairs)


def swapped(value):
    return lax.ppermute(value, "core", [(0, 1), (1, 0)])


def together(first, second):
    return lax.optimization_barrier((first, second))


def halves(value):
    high = value.astype(jnp.bfloat16)
    low = (value - high.astype(jnp.float32)).astype(jnp.bfloat16)
    return high, low


def times(left, right, dims):
    return lax.dot_general(left, right, (dims, ((), ())), preferred_element_type=jnp.float32)


def forward_kernel(count, core_ref, *refs):
    foot_own, foot_other = refs[:count], refs[count:2 * count]
    flux_own, flux_other = refs[2 * count:2 * count + 2]
    outs = refs[2 * count + 2:3 * count + 2]
    high_ref, low_ref = refs[3 * count + 2:]
    rows, cells = foot_own[0].shape[-2:]

    @pl.when(pl.program_id(0) == 0)
    def _():
        for i in range(count):
            for side, source in ((0, foot_own[i]), (1, foot_other[i])):
                high, low = halves(source[...].reshape(rows, cells))
                at = (pl.ds(i * rows, rows), pl.ds(side * cells, cells))
                high_ref[at] = high
                low_ref[at] = low

    total = None
    for side, source in ((0, flux_own), (1, flux_other)):
        high, low = halves(source[...].reshape(cells, -1))
        at = pl.ds(side * cells, cells)
        dims = ((1,), (0,))
        term = times(high_ref[:, at], high, dims)
        term = term + times(low_ref[:, at], high, dims)
        term = term + times(high_ref[:, at], low, dims)
        total = term if total is None else total + term
    for i in range(count):
        outs[i][...] = total[i * rows:(i + 1) * rows]


def forward(
    foot_own, own_specs, foot_other, other_specs, rows, flux, flux_other, cells, half, core
):
    count = len(foot_own)
    tile = min(WIDE, half)
    steps = half // tile
    outs = pl.pallas_call(
        functools.partial(forward_kernel, count),
        grid_spec=pltpu.PrefetchScalarGridSpec(
            num_scalar_prefetch=1,
            grid=(steps,),
            in_specs=[
                *own_specs,
                *other_specs,
                pl.BlockSpec((1, cells, tile), lambda j, c: (0, 0, c[0] * steps + j)),
                pl.BlockSpec((cells, tile), lambda j, c: (0, j)),
            ],
            out_specs=[pl.BlockSpec((rows, tile), lambda j, c: (0, j))] * count,
            scratch_shapes=[pltpu.VMEM((count * rows, 2 * cells), jnp.bfloat16)] * 2,
        ),
        out_shape=[jax.ShapeDtypeStruct((rows, half), jnp.float32)] * count,
        compiler_params=pltpu.CompilerParams(vmem_limit_bytes=VMEM_LIMIT),
        cost_estimate=LIGHT,
    )(core, *foot_own, *foot_other, flux, flux_other)
    return list(outs)


def adjoint_kernel(count, sides, first, core_ref, *refs):
    weighted, refs = refs[:count], refs[count:]
    foot, refs = refs[:sides * count], refs[sides * count:]
    before, refs = (None, refs) if first else (refs[:sides], refs[sides:])
    outs, (high_ref, low_ref) = refs[:sides], refs[sides:]
    rows, tile = foot[0].shape[-2:]

    @pl.when(pl.program_id(0) == 0)
    def _():
        for i in range(count):
            high, low = halves(weighted[i][...])
            high_ref[pl.ds(i * rows, rows), :] = high
            low_ref[pl.ds(i * rows, rows), :] = low

    for side in range(sides):
        mine = foot[side * count:(side + 1) * count]
        slab = jnp.concatenate([ref[...].reshape(rows, tile) for ref in mine], axis=0)
        high, low = halves(slab)
        dims = ((0,), (0,))
        total = times(high, high_ref[...], dims)
        total = total + times(low, high_ref[...], dims)
        total = total + times(high, low_ref[...], dims)
        if not first:
            total = total + before[side][...]
        outs[side][...] = total


def adjoint(weighted, sides, core, cells):
    count = len(weighted)
    rows, half = weighted[0].shape
    tile = min(TILE, cells)
    first = sides[0][2] is None
    out_specs = []
    for side in sides:
        if side[4]:
            out_specs.append(pl.BlockSpec((tile, half), lambda j, c: (j, c[0])))
        else:
            out_specs.append(pl.BlockSpec((tile, half), lambda j, c: (j, 0)))
    foot = [array for side in sides for array in side[0]]
    earlier = [] if first else [side[2] for side in sides]
    at = 1 + count + len(foot)
    return pl.pallas_call(
        functools.partial(adjoint_kernel, count, len(sides), first),
        grid_spec=pltpu.PrefetchScalarGridSpec(
            num_scalar_prefetch=1,
            grid=(cells // tile,),
            in_specs=[
                *[pl.BlockSpec((rows, half), lambda j, c: (0, 0))] * count,
                *[spec(tile) for side in sides for spec in side[1]],
                *([] if first else out_specs),
            ],
            out_specs=out_specs,
            scratch_shapes=[pltpu.VMEM((count * rows, half), jnp.bfloat16)] * 2,
        ),
        out_shape=[jax.ShapeDtypeStruct((cells, side[3]), jnp.float32) for side in sides],
        input_output_aliases={} if first else {at + i: i for i in range(len(sides))},
        compiler_params=pltpu.CompilerParams(vmem_limit_bytes=VMEM_LIMIT),
        cost_estimate=LIGHT,
    )(core, *weighted, *foot, *earlier)


def cut_kernel(*refs):
    count = len(refs) // 2
    for source, out in zip(refs[:count], refs[count:]):
        out[...] = source[0, 0]


def cut(footprint, later, rows, r):
    cells = footprint.shape[3]
    tile = min(TILE, cells)
    return list(pl.pallas_call(
        cut_kernel,
        grid=(cells // tile,),
        in_specs=[pl.BlockSpec((1, 1, rows, tile), lambda j, lag=lag: (0, lag, r, j)) for lag in later],
        out_specs=[pl.BlockSpec((rows, tile), lambda j: (0, j))] * len(later),
        out_shape=[jax.ShapeDtypeStruct((rows, cells), jnp.float32)] * len(later),
        cost_estimate=LIGHT,
    )(*[footprint] * len(later)))


def pair_kernel(core_ref, flux, foot, out):
    cells = flux.shape[1]
    slots = foot.shape[2]
    out[pl.ds(0, cells), :] = flux[0]
    out[pl.ds(out.shape[0] - slots, slots), :] = foot[0, 0]


def pair(flux, footprint, half, foot_at, core):
    _, _, slots, cells = footprint.shape
    tile = min(TILE, half)
    steps = half // tile
    return pl.pallas_call(
        pair_kernel,
        grid_spec=pltpu.PrefetchScalarGridSpec(
            num_scalar_prefetch=1,
            grid=(steps,),
            in_specs=[
                pl.BlockSpec((1, cells, tile), lambda j, c: (0, 0, (1 - c[0]) * steps + j)),
                pl.BlockSpec((1, 1, slots, tile), lambda j, c: (0, 0, 0, j)),
            ],
            out_specs=pl.BlockSpec((foot_at + slots, tile), lambda j, c: (0, j)),
        ),
        out_shape=jax.ShapeDtypeStruct((foot_at + slots, half), jnp.float32),
        cost_estimate=LIGHT,
    )(core, flux, footprint)


def combine_kernel(scale, same, *refs):
    total = same[...]
    for ref in refs[:-1]:
        total = total + ref[...]
    refs[-1][...] = scale[...] * total


def combine(scale, same, gathered, r):
    rows, half = gathered[0].shape
    tile = min(WIDE, half)
    block = pl.BlockSpec((rows, tile), lambda j: (0, j))
    return pl.pallas_call(
        combine_kernel,
        grid=(half // tile,),
        in_specs=[
            pl.BlockSpec((rows, 1), lambda j: (r, 0)),
            block,
            *[block] * len(gathered),
        ],
        out_specs=block,
        out_shape=jax.ShapeDtypeStruct((rows, half), jnp.float32),
        cost_estimate=LIGHT,
    )(scale, same, *gathered)


def paste_kernel(core_ref, arrived, before, out_ref):
    out_ref[...] = arrived[...]


def paste(arrived, whole, core):
    cells, half = arrived.shape
    tile = min(TILE, cells)
    return pl.pallas_call(
        paste_kernel,
        grid_spec=pltpu.PrefetchScalarGridSpec(
            num_scalar_prefetch=1,
            grid=(cells // tile,),
            in_specs=[
                pl.BlockSpec((tile, half), lambda j, c: (j, 0)),
                pl.BlockSpec(memory_space=pl.ANY),
            ],
            out_specs=pl.BlockSpec((tile, half), lambda j, c: (j, 1 - c[0])),
        ),
        out_shape=jax.ShapeDtypeStruct(whole.shape, jnp.float32),
        input_output_aliases={2: 0},
        cost_estimate=LIGHT,
    )(core, arrived, whole)


def on_device(footprint, flux, obs_weight, obs_count):
    _, lags, slots, cells = footprint.shape
    half = flux.shape[2] // 2
    rows = slots // CHUNKS
    core_at = lax.axis_index("core")
    core = core_at.astype(jnp.int32)[None]
    valid = (jnp.arange(slots, dtype=jnp.int32) < obs_count[0]).astype(jnp.float32)
    row_scale = (valid * obs_weight[0])[:, None]
    later = range(1, lags)

    def whole(block):
        return pl.BlockSpec((rows, cells), lambda j, c: (block, 0))

    def column(block):
        return lambda tile: pl.BlockSpec((rows, tile), lambda j, c: (block, j))

    pieces = cut(footprint, later, rows, 0)
    own = [[shifted(piece, -lag) for piece, lag in zip(pieces, later)]]
    if half == cells:
        foot_at = pl.cdiv(cells, rows)
        after, _ = together(flux, pieces[0])
        flux_other = foot_other = swapped(pair(after, footprint, half, foot_at * rows, core))
    else:
        flux_other = swapped(lax.dynamic_slice_in_dim(flux[0], (1 - core_at) * half, half, 1))
        foot_other = swapped(footprint[0, 0])
        foot_at = 0
    chunks = range(CHUNKS)
    same = forward(
        [footprint] * CHUNKS,
        [pl.BlockSpec((1, 1, rows, cells), lambda j, c, r=r: (0, 0, r, 0)) for r in chunks],
        [foot_other] * CHUNKS,
        [whole(foot_at + r) for r in chunks],
        rows, flux, flux_other, cells, half, core,
    )
    chunk_specs = [whole(0)] * len(later)

    other, terms, weighted = [], [], []

    def gather_up(r):
        arrived = [shifted(terms[r][lag - 1], lag) for lag in later]
        if r > 0:
            same[r], weighted[r - 1] = together(same[r], weighted[r - 1])
        total = combine(row_scale, same[r], arrived, r)
        if r > 0:
            total, weighted[r - 1] = together(total, weighted[r - 1])
        return total

    for r in chunks:
        if r > 0:
            pieces = cut(footprint, later, rows, r)
            for i in range(len(later)):
                pieces[i], own[r - 1][i] = together(pieces[i], own[r - 1][i])
            own.append([shifted(piece, -lag) for piece, lag in zip(pieces, later)])
            for i in range(len(later)):
                own[r][i], terms[r - 1][i] = together(own[r][i], terms[r - 1][i])
        other.append([swapped(value) for value in own[r]])
        if r > 0:
            total = gather_up(r - 1)
            for i in range(len(later)):
                other[r][i], total = together(other[r][i], total)
            weighted.append(lax.psum(total, "z"))
        terms.append(forward(
            own[r], chunk_specs, other[r], chunk_specs,
            rows, flux, flux_other, cells, half, core,
        ))

    def my_side(r, before):
        first = pl.BlockSpec((1, 1, rows, min(TILE, cells)), lambda j, c: (0, 0, r, j))
        specs = [lambda tile: first] + [column(0)] * len(later)
        return [footprint, *own[r]], specs, before, 2 * half, True

    def their_side(r, before):
        specs = [column(foot_at + r)] + [column(0)] * len(later)
        return [foot_other, *other[r]], specs, before, half, False

    def spread(value):
        return [value] + [shifted(value, -lag) for lag in later]

    weighted.append(lax.psum(gather_up(CHUNKS - 1), "z"))
    mine, theirs = None, None
    for r in chunks:
        if r > 1:
            weighted[r], mine = together(weighted[r], mine)
        if r > 0:
            here = spread(weighted[r - 1])
            mine, theirs = adjoint(here, [my_side(r - 1, mine), their_side(r - 1, theirs)], core, cells)
    here = spread(weighted[r])
    (theirs,) = adjoint(here, [their_side(r, theirs)], core, cells)
    (mine,) = adjoint(here, [my_side(r, mine)], core, cells)
    return paste(swapped(theirs), mine, core)[None]


def solution(mesh):
    devices = mesh.devices
    split = Mesh(devices.reshape(devices.shape[0], devices.shape[1] // 2, 2), ("tm", "z", "core"))
    cells = ("z", "core")
    placed = (P("tm", None, None, cells), P("tm", cells, None), P("tm", None), P("tm"))
    return jax.shard_map(
        on_device, mesh=split, in_specs=placed, out_specs=P("tm", cells, None), check_vma=False
    )
```

```python
import functools

import jax
import jax.numpy as jnp
from jax import lax
from jax.experimental import pallas as pl
from jax.experimental.pallas import tpu as pltpu
from jax.sharding import Mesh, PartitionSpec as P

CHUNKS = 4
TILE = 256
WIDE = 512
LIGHT = pl.CostEstimate(flops=1, bytes_accessed=1, transcendentals=0)
VMEM_LIMIT = 60 * 1024 * 1024


def shifted(value, by):
    devices = lax.axis_size("tm")
    pairs = [(i, i + by) for i in range(devices) if 0 <= i + by < devices]
    return lax.ppermute(value, "tm", pairs)


def swapped(value):
    return lax.ppermute(value, "core", [(0, 1), (1, 0)])


def together(first, second):
    return lax.optimization_barrier((first, second))


def halves(value):
    high = value.astype(jnp.bfloat16)
    low = (value - high.astype(jnp.float32)).astype(jnp.bfloat16)
    return high, low


def times(left, right, dims):
    return lax.dot_general(left, right, (dims, ((), ())), preferred_element_type=jnp.float32)


def split_kernel(core_ref, own, other, high_ref, low_ref):
    cells = other.shape[0]
    for at, value in ((0, own[0]), (cells, other[...])):
        high, low = halves(value)
        high_ref[pl.ds(at, cells), :] = high
        low_ref[pl.ds(at, cells), :] = low


def split(flux, flux_other, core):
    cells, half = flux_other.shape
    tile = min(TILE, half)
    steps = half // tile
    block = pl.BlockSpec((2 * cells, tile), lambda j, c: (0, j))
    return pl.pallas_call(
        split_kernel,
        grid_spec=pltpu.PrefetchScalarGridSpec(
            num_scalar_prefetch=1,
            grid=(steps,),
            in_specs=[
                pl.BlockSpec((1, cells, tile), lambda j, c: (0, 0, c[0] * steps + j)),
                pl.BlockSpec((cells, tile), lambda j, c: (0, j)),
            ],
            out_specs=[block, block],
        ),
        out_shape=[jax.ShapeDtypeStruct((2 * cells, half), jnp.bfloat16)] * 2,
        cost_estimate=LIGHT,
    )(core, flux, flux_other)


def forward_kernel(count, *refs):
    foot_own, foot_other = refs[:count], refs[count:2 * count]
    flux_high, flux_low = refs[2 * count:2 * count + 2]
    outs = refs[2 * count + 2:3 * count + 2]
    high_ref, low_ref = refs[3 * count + 2:]
    rows, cells = foot_own[0].shape[-2:]

    @pl.when(pl.program_id(0) == 0)
    def _():
        for i in range(count):
            for side, source in ((0, foot_own[i]), (1, foot_other[i])):
                high, low = halves(source[...].reshape(rows, cells))
                at = (pl.ds(i * rows, rows), pl.ds(side * cells, cells))
                high_ref[at] = high
                low_ref[at] = low

    dims = ((1,), (0,))
    total = times(high_ref[...], flux_high[...], dims)
    total = total + times(low_ref[...], flux_high[...], dims)
    total = total + times(high_ref[...], flux_low[...], dims)
    for i in range(count):
        outs[i][...] = total[i * rows:(i + 1) * rows]


def forward(foot_own, own_specs, foot_other, other_specs, rows, flux_parts):
    count = len(foot_own)
    depth, half = flux_parts[0].shape
    tile = min(WIDE, half)
    outs = pl.pallas_call(
        functools.partial(forward_kernel, count),
        grid=(half // tile,),
        in_specs=[
            *own_specs,
            *other_specs,
            *[pl.BlockSpec((depth, tile), lambda j: (0, j))] * 2,
        ],
        out_specs=[pl.BlockSpec((rows, tile), lambda j: (0, j))] * count,
        scratch_shapes=[pltpu.VMEM((count * rows, depth), jnp.bfloat16)] * 2,
        out_shape=[jax.ShapeDtypeStruct((rows, half), jnp.float32)] * count,
        compiler_params=pltpu.CompilerParams(vmem_limit_bytes=VMEM_LIMIT),
        cost_estimate=LIGHT,
    )(*foot_own, *foot_other, *flux_parts)
    return list(outs)


def adjoint_kernel(count, sides, first, core_ref, *refs):
    weighted, refs = refs[:count], refs[count:]
    foot, refs = refs[:sides * count], refs[sides * count:]
    before, refs = (None, refs) if first else (refs[:sides], refs[sides:])
    outs, (high_ref, low_ref) = refs[:sides], refs[sides:]
    rows, tile = foot[0].shape[-2:]

    @pl.when(pl.program_id(0) == 0)
    def _():
        for i in range(count):
            high, low = halves(weighted[i][...])
            high_ref[pl.ds(i * rows, rows), :] = high
            low_ref[pl.ds(i * rows, rows), :] = low

    for side in range(sides):
        mine = foot[side * count:(side + 1) * count]
        slab = jnp.concatenate([ref[...].reshape(rows, tile) for ref in mine], axis=0)
        high, low = halves(slab.T)
        dims = ((1,), (0,))
        total = times(high, high_ref[...], dims)
        total = total + times(low, high_ref[...], dims)
        total = total + times(high, low_ref[...], dims)
        if not first:
            total = total + before[side][...]
        outs[side][...] = total


def adjoint(weighted, sides, core, cells):
    count = len(weighted)
    rows, half = weighted[0].shape
    tile = min(WIDE, cells)
    first = sides[0][2] is None
    out_specs = []
    for side in sides:
        if side[4]:
            out_specs.append(pl.BlockSpec((tile, half), lambda j, c: (j, c[0])))
        else:
            out_specs.append(pl.BlockSpec((tile, half), lambda j, c: (j, 0)))
    foot = [array for side in sides for array in side[0]]
    earlier = [] if first else [side[2] for side in sides]
    at = 1 + count + len(foot)
    return pl.pallas_call(
        functools.partial(adjoint_kernel, count, len(sides), first),
        grid_spec=pltpu.PrefetchScalarGridSpec(
            num_scalar_prefetch=1,
            grid=(cells // tile,),
            in_specs=[
                *[pl.BlockSpec((rows, half), lambda j, c: (0, 0))] * count,
                *[spec(tile) for side in sides for spec in side[1]],
                *([] if first else out_specs),
            ],
            out_specs=out_specs,
            scratch_shapes=[pltpu.VMEM((count * rows, half), jnp.bfloat16)] * 2,
        ),
        out_shape=[jax.ShapeDtypeStruct((cells, side[3]), jnp.float32) for side in sides],
        input_output_aliases={} if first else {at + i: i for i in range(len(sides))},
        compiler_params=pltpu.CompilerParams(vmem_limit_bytes=VMEM_LIMIT),
        cost_estimate=LIGHT,
    )(core, *weighted, *foot, *earlier)


def cut_kernel(*refs):
    count = len(refs) // 2
    for source, out in zip(refs[:count], refs[count:]):
        out[...] = source[0, 0]


def cut(footprint, lags, rows, r):
    cells = footprint.shape[3]
    tile = min(WIDE, cells)
    return list(pl.pallas_call(
        cut_kernel,
        grid=(cells // tile,),
        in_specs=[pl.BlockSpec((1, 1, rows, tile), lambda j, lag=lag: (0, lag, r, j)) for lag in lags],
        out_specs=[pl.BlockSpec((rows, tile), lambda j: (0, j))] * len(lags),
        out_shape=[jax.ShapeDtypeStruct((rows, cells), jnp.float32)] * len(lags),
        cost_estimate=LIGHT,
    )(*[footprint] * len(lags)))


def stack_kernel(*refs):
    for i, ref in enumerate(refs[:-1]):
        rows = ref.shape[0]
        refs[-1][pl.ds(i * rows, rows), :] = ref[...]


def stack(pieces):
    rows, cells = pieces[0].shape
    tile = min(WIDE, cells)
    return pl.pallas_call(
        stack_kernel,
        grid=(cells // tile,),
        in_specs=[pl.BlockSpec((rows, tile), lambda j: (0, j))] * len(pieces),
        out_specs=pl.BlockSpec((rows * len(pieces), tile), lambda j: (0, j)),
        out_shape=jax.ShapeDtypeStruct((rows * len(pieces), cells), jnp.float32),
        cost_estimate=LIGHT,
    )(*pieces)


def side_kernel(core_ref, flux, out):
    out[...] = flux[0]


def side_of(flux, core):
    _, cells, width = flux.shape
    tile = min(WIDE, width // 2)
    steps = width // 2 // tile
    return pl.pallas_call(
        side_kernel,
        grid_spec=pltpu.PrefetchScalarGridSpec(
            num_scalar_prefetch=1,
            grid=(steps,),
            in_specs=[pl.BlockSpec((1, cells, tile), lambda j, c: (0, 0, (1 - c[0]) * steps + j))],
            out_specs=pl.BlockSpec((cells, tile), lambda j, c: (0, j)),
        ),
        out_shape=jax.ShapeDtypeStruct((cells, width // 2), jnp.float32),
        cost_estimate=LIGHT,
    )(core, flux)


def combine_kernel(scale, same, *refs):
    total = same[...]
    for ref in refs[:-1]:
        total = total + ref[...]
    refs[-1][...] = scale[...] * total


def combine(scale, same, gathered, r):
    rows, half = gathered[0].shape
    tile = min(WIDE, half)
    block = pl.BlockSpec((rows, tile), lambda j: (0, j))
    return pl.pallas_call(
        combine_kernel,
        grid=(half // tile,),
        in_specs=[
            pl.BlockSpec((rows, 1), lambda j: (r, 0)),
            block,
            *[block] * len(gathered),
        ],
        out_specs=block,
        out_shape=jax.ShapeDtypeStruct((rows, half), jnp.float32),
        cost_estimate=LIGHT,
    )(scale, same, *gathered)


def paste_kernel(core_ref, arrived, before, out_ref):
    out_ref[...] = arrived[...]


def paste(arrived, whole, core):
    cells, half = arrived.shape
    tile = min(TILE, cells)
    return pl.pallas_call(
        paste_kernel,
        grid_spec=pltpu.PrefetchScalarGridSpec(
            num_scalar_prefetch=1,
            grid=(cells // tile,),
            in_specs=[
                pl.BlockSpec((tile, half), lambda j, c: (j, 0)),
                pl.BlockSpec(memory_space=pl.ANY),
            ],
            out_specs=pl.BlockSpec((tile, half), lambda j, c: (j, 1 - c[0])),
        ),
        out_shape=jax.ShapeDtypeStruct(whole.shape, jnp.float32),
        input_output_aliases={2: 0},
        cost_estimate=LIGHT,
    )(core, arrived, whole)


def on_device(footprint, flux, obs_weight, obs_count):
    _, lags, slots, cells = footprint.shape
    half = flux.shape[2] // 2
    rows = slots // CHUNKS
    chunks = range(CHUNKS)
    core = lax.axis_index("core").astype(jnp.int32)[None]
    valid = (jnp.arange(slots, dtype=jnp.int32) < obs_count[0]).astype(jnp.float32)
    row_scale = (valid * obs_weight[0])[:, None]
    later = range(1, lags)

    pieces = cut(footprint, later, rows, 0)
    own = [[shifted(piece, -lag) for piece, lag in zip(pieces, later)]]
    after, _ = together(flux, pieces[0])
    flux_parts = split(flux, swapped(side_of(after, core)), core)
    foot_other = swapped(cut(footprint, [0], slots, 0)[0])
    same = forward(
        [footprint] * CHUNKS,
        [pl.BlockSpec((1, 1, rows, cells), lambda j, r=r: (0, 0, r, 0)) for r in chunks],
        [foot_other] * CHUNKS,
        [pl.BlockSpec((rows, cells), lambda j, r=r: (r, 0)) for r in chunks],
        rows, flux_parts,
    )
    specs = [pl.BlockSpec((rows, cells), lambda j: (0, 0))] * len(later)

    other_specs = [pl.BlockSpec((rows, cells), lambda j, i=i: (i, 0)) for i in range(len(later))]

    other, terms, weighted, sent = [], [], [], []

    def gather_up(r):
        arrived = [shifted(terms[r][lag - 1], lag) for lag in later]
        if r + 1 < CHUNKS:
            arrived[0], terms[r + 1][0] = together(arrived[0], terms[r + 1][0])
        total = combine(row_scale, same[r], arrived, r)
        if r > 0:
            total, weighted[r - 1] = together(total, weighted[r - 1])
        return total

    def column(r):
        return lambda tile: pl.BlockSpec((rows, tile), lambda j, c: (r, j))

    def my_side(r, before):
        def first(tile):
            return pl.BlockSpec((1, 1, rows, tile), lambda j, c: (0, 0, r, j))

        return [footprint, *own[r]], [first] + [column(0)] * len(later), before, 2 * half, True

    def their_side(r, before):
        foot = [foot_other] + [other[r]] * len(later)
        return foot, [column(r)] + [column(i) for i in range(len(later))], before, half, False

    done = [None, None]

    def advance(r):
        total = gather_up(r)
        arrived = lax.psum(total, "z")
        if r > 0:
            for i in range(len(later)):
                arrived, sent[r - 1][i] = together(arrived, sent[r - 1][i])
        if r > 1:
            arrived, done[0] = together(arrived, done[0])
        weighted.append(arrived)
        sent.append([shifted(arrived, -lag) for lag in later])
        if r > 0:
            first, weighted[r] = together(weighted[r - 1], weighted[r])
            both = [my_side(r - 1, done[0]), their_side(r - 1, done[1])]
            done[:] = adjoint([first, *sent[r - 1]], both, core, cells)
        return total

    for r in chunks:
        if r > 0:
            pieces = cut(footprint, later, rows, r)
            for i in range(len(later)):
                pieces[i], own[r - 1][i] = together(pieces[i], own[r - 1][i])
            own.append([shifted(piece, -lag) for piece, lag in zip(pieces, later)])
            for i in range(len(later)):
                own[r][i], terms[r - 1][i] = together(own[r][i], terms[r - 1][i])
        if r > 1:
            total = advance(r - 2)
            for i in range(len(later)):
                own[r][i], _ = together(own[r][i], total)
        other.append(swapped(stack(own[r])))
        terms.append(forward(own[r], specs, [other[r]] * len(later), other_specs, rows, flux_parts))
    for r in range(max(CHUNKS - 2, 0), CHUNKS):
        advance(r)
    mine, theirs = done
    here = [weighted[r], *sent[r]]
    (theirs,) = adjoint(here, [their_side(r, theirs)], core, cells)
    (mine,) = adjoint(here, [my_side(r, mine)], core, cells)
    return paste(swapped(theirs), mine, core)[None]


def solution(mesh):
    devices = mesh.devices
    split = Mesh(devices.reshape(devices.shape[0], devices.shape[1] // 2, 2), ("tm", "z", "core"))
    cells = ("z", "core")
    placed = (P("tm", None, None, cells), P("tm", cells, None), P("tm", None), P("tm"))
    return jax.shard_map(
        on_device, mesh=split, in_specs=placed, out_specs=P("tm", cells, None), check_vma=False
    )
```

```python
import functools

import jax
import jax.numpy as jnp
from jax import lax
from jax.experimental import pallas as pl
from jax.experimental.pallas import tpu as pltpu
from jax.sharding import Mesh, PartitionSpec as P

CHUNKS = 4
TILE = 256
WIDE = 512
LIGHT = pl.CostEstimate(flops=1, bytes_accessed=1, transcendentals=0)
VMEM_LIMIT = 60 * 1024 * 1024


def shifted(value, by):
    devices = lax.axis_size("tm")
    pairs = [(i, i + by) for i in range(devices) if 0 <= i + by < devices]
    return lax.ppermute(value, "tm", pairs)


def cycled(value, by):
    devices = lax.axis_size("tm")
    return lax.ppermute(value, "tm", [(i, (i - by) % devices) for i in range(devices)])


def swapped(value):
    return lax.ppermute(value, "core", [(0, 1), (1, 0)])


def together(first, second):
    return lax.optimization_barrier((first, second))


def halves(value):
    high = value.astype(jnp.bfloat16)
    low = (value - high.astype(jnp.float32)).astype(jnp.bfloat16)
    return high, low


def times(left, right, dims):
    return lax.dot_general(left, right, (dims, ((), ())), preferred_element_type=jnp.float32)


def split_kernel(core_ref, own, other, high_ref, low_ref):
    cells = other.shape[0]
    for at, value in ((0, own[0]), (cells, other[...])):
        high, low = halves(value)
        high_ref[pl.ds(at, cells), :] = high
        low_ref[pl.ds(at, cells), :] = low


def split(flux, flux_other, core):
    cells, half = flux_other.shape
    tile = min(TILE, half)
    steps = half // tile
    block = pl.BlockSpec((2 * cells, tile), lambda j, c: (0, j))
    return pl.pallas_call(
        split_kernel,
        grid_spec=pltpu.PrefetchScalarGridSpec(
            num_scalar_prefetch=1,
            grid=(steps,),
            in_specs=[
                pl.BlockSpec((1, cells, tile), lambda j, c: (0, 0, c[0] * steps + j)),
                pl.BlockSpec((cells, tile), lambda j, c: (0, j)),
            ],
            out_specs=[block, block],
        ),
        out_shape=[jax.ShapeDtypeStruct((2 * cells, half), jnp.bfloat16)] * 2,
        name="split",
        cost_estimate=LIGHT,
    )(core, flux, flux_other)


def forward_kernel(count, *refs):
    foot_own, foot_other = refs[:count], refs[count:2 * count]
    flux_high, flux_low = refs[2 * count:2 * count + 2]
    outs = refs[2 * count + 2:3 * count + 2]
    parts_ref = refs[-1]
    rows, cells = foot_own[0].shape[-2:]
    depth = count * rows

    @pl.when(pl.program_id(0) == 0)
    def _():
        for i in range(count):
            for side, source in ((0, foot_own[i]), (1, foot_other[i])):
                high, low = halves(source[...].reshape(rows, cells))
                columns = pl.ds(side * cells, cells)
                parts_ref[pl.ds(i * rows, rows), columns] = high
                parts_ref[pl.ds(depth + i * rows, rows), columns] = low

    dims = ((1,), (0,))
    both = times(parts_ref[...], flux_high[...], dims)
    total = both[:depth] + both[depth:] + times(parts_ref[pl.ds(0, depth), :], flux_low[...], dims)
    for i in range(count):
        outs[i][...] = total[i * rows:(i + 1) * rows]


def forward(foot_own, own_specs, foot_other, other_specs, rows, flux_parts):
    count = len(foot_own)
    depth, half = flux_parts[0].shape
    tile = min(WIDE, half)
    outs = pl.pallas_call(
        functools.partial(forward_kernel, count),
        grid=(half // tile,),
        in_specs=[
            *own_specs,
            *other_specs,
            *[pl.BlockSpec((depth, tile), lambda j: (0, j))] * 2,
        ],
        out_specs=[pl.BlockSpec((rows, tile), lambda j: (0, j))] * count,
        scratch_shapes=[pltpu.VMEM((2 * count * rows, depth), jnp.bfloat16)],
        out_shape=[jax.ShapeDtypeStruct((rows, half), jnp.float32)] * count,
        compiler_params=pltpu.CompilerParams(vmem_limit_bytes=VMEM_LIMIT),
        name="forward",
        cost_estimate=LIGHT,
    )(*foot_own, *foot_other, *flux_parts)
    return list(outs)


def adjoint_kernel(count, sides, first, place_ref, *refs):
    weighted, refs = refs[:count], refs[count:]
    foot, refs = refs[:sides * count], refs[sides * count:]
    before, refs = (None, refs) if first else (refs[:sides], refs[sides:])
    outs, (high_ref, low_ref) = refs[:sides], refs[sides:]
    rows, tile = foot[0].shape[-2:]

    @pl.when(pl.program_id(0) == 0)
    def _():
        for i in range(count):
            value = jnp.where(place_ref[1] + i < place_ref[2], weighted[i][...], 0.0)
            high, low = halves(value)
            high_ref[pl.ds(i * rows, rows), :] = high
            low_ref[pl.ds(i * rows, rows), :] = low

    dims = ((1,), (0,))
    for side in range(sides):
        mine = foot[side * count:(side + 1) * count]
        slab = jnp.concatenate([ref[...].reshape(rows, tile) for ref in mine], axis=0)
        high, low = halves(slab.T)
        both = times(jnp.concatenate([high, low], axis=0), high_ref[...], dims)
        total = both[:tile] + both[tile:] + times(high, low_ref[...], dims)
        if not first:
            total = total + before[side][...]
        outs[side][...] = total


def adjoint(weighted, sides, core, cells):
    count = len(weighted)
    rows, half = weighted[0].shape
    tile = min(WIDE, cells)
    first = sides[0][2] is None
    out_specs = []
    for side in sides:
        if side[4]:
            out_specs.append(pl.BlockSpec((tile, half), lambda j, c: (j, c[0])))
        else:
            out_specs.append(pl.BlockSpec((tile, half), lambda j, c: (j, 0)))
    foot = [array for side in sides for array in side[0]]
    earlier = [] if first else [side[2] for side in sides]
    at = 1 + count + len(foot)
    return pl.pallas_call(
        functools.partial(adjoint_kernel, count, len(sides), first),
        grid_spec=pltpu.PrefetchScalarGridSpec(
            num_scalar_prefetch=1,
            grid=(cells // tile,),
            in_specs=[
                *[pl.BlockSpec((rows, half), lambda j, c: (0, 0))] * count,
                *[spec(tile) for side in sides for spec in side[1]],
                *([] if first else out_specs),
            ],
            out_specs=out_specs,
            scratch_shapes=[pltpu.VMEM((count * rows, half), jnp.bfloat16)] * 2,
        ),
        out_shape=[jax.ShapeDtypeStruct((cells, side[3]), jnp.float32) for side in sides],
        input_output_aliases={} if first else {at + i: i for i in range(len(sides))},
        compiler_params=pltpu.CompilerParams(vmem_limit_bytes=VMEM_LIMIT),
        name="adjoint",
        cost_estimate=LIGHT,
    )(core, *weighted, *foot, *earlier)


def cut_kernel(*refs):
    count = len(refs) // 2
    for source, out in zip(refs[:count], refs[count:]):
        out[...] = source[0, 0]


def cut(footprint, lags, rows, r):
    cells = footprint.shape[3]
    tile = min(WIDE, cells)
    return list(pl.pallas_call(
        cut_kernel,
        grid=(cells // tile,),
        in_specs=[pl.BlockSpec((1, 1, rows, tile), lambda j, lag=lag: (0, lag, r, j)) for lag in lags],
        out_specs=[pl.BlockSpec((rows, tile), lambda j: (0, j))] * len(lags),
        out_shape=[jax.ShapeDtypeStruct((rows, cells), jnp.float32)] * len(lags),
        name="cut",
        cost_estimate=LIGHT,
    )(*[footprint] * len(lags)))


def stack_kernel(*refs):
    for i, ref in enumerate(refs[:-1]):
        rows = ref.shape[0]
        refs[-1][pl.ds(i * rows, rows), :] = ref[...]


def stack(pieces):
    rows, cells = pieces[0].shape
    tile = min(WIDE, cells)
    return pl.pallas_call(
        stack_kernel,
        grid=(cells // tile,),
        in_specs=[pl.BlockSpec((rows, tile), lambda j: (0, j))] * len(pieces),
        out_specs=pl.BlockSpec((rows * len(pieces), tile), lambda j: (0, j)),
        out_shape=jax.ShapeDtypeStruct((rows * len(pieces), cells), jnp.float32),
        name="stack",
        cost_estimate=LIGHT,
    )(*pieces)


def side_kernel(core_ref, flux, out):
    out[...] = flux[0]


def side_of(flux, core):
    _, cells, width = flux.shape
    tile = min(WIDE, width // 2)
    steps = width // 2 // tile
    return pl.pallas_call(
        side_kernel,
        grid_spec=pltpu.PrefetchScalarGridSpec(
            num_scalar_prefetch=1,
            grid=(steps,),
            in_specs=[pl.BlockSpec((1, cells, tile), lambda j, c: (0, 0, (1 - c[0]) * steps + j))],
            out_specs=pl.BlockSpec((cells, tile), lambda j, c: (0, j)),
        ),
        out_shape=jax.ShapeDtypeStruct((cells, width // 2), jnp.float32),
        name="side",
        cost_estimate=LIGHT,
    )(core, flux)


def combine_kernel(place_ref, scale, same, *refs):
    total = same[...]
    for lag, ref in enumerate(refs[:-1], 1):
        total = total + jnp.where(place_ref[1] >= lag, ref[...], 0.0)
    refs[-1][...] = scale[...] * total


def combine(scale, same, arrived, r, place):
    rows, half = same.shape
    tile = min(WIDE, half)
    block = pl.BlockSpec((rows, tile), lambda j, c: (0, j))
    return pl.pallas_call(
        combine_kernel,
        grid_spec=pltpu.PrefetchScalarGridSpec(
            num_scalar_prefetch=1,
            grid=(half // tile,),
            in_specs=[
                pl.BlockSpec((rows, 1), lambda j, c: (r, 0)),
                block,
                *[block] * len(arrived),
            ],
            out_specs=block,
        ),
        out_shape=jax.ShapeDtypeStruct((rows, half), jnp.float32),
        name="combine",
        cost_estimate=LIGHT,
    )(place, scale, same, *arrived)


def choose_kernel(place_ref, *refs):
    count = len(refs) // 3
    for i in range(count):
        down, up, out = refs[i], refs[count + i], refs[2 * count + i]
        out[...] = jnp.where(place_ref[1] > i, down[...].reshape(out.shape), up[...])


def choose(place, down, down_specs, up):
    rows, width = up[0].shape
    tile = min(WIDE, width)
    block = pl.BlockSpec((rows, tile), lambda j, c: (0, j))
    return list(pl.pallas_call(
        choose_kernel,
        grid_spec=pltpu.PrefetchScalarGridSpec(
            num_scalar_prefetch=1,
            grid=(width // tile,),
            in_specs=[*[spec(tile) for spec in down_specs], *[block] * len(up)],
            out_specs=[block] * len(up),
        ),
        out_shape=[jax.ShapeDtypeStruct((rows, width), jnp.float32)] * len(up),
        name="choose",
        cost_estimate=LIGHT,
    )(place, *down, *up))


def paste_kernel(core_ref, arrived, before, out_ref):
    out_ref[...] = arrived[...]


def paste(arrived, whole, core):
    cells, half = arrived.shape
    tile = min(TILE, cells)
    return pl.pallas_call(
        paste_kernel,
        grid_spec=pltpu.PrefetchScalarGridSpec(
            num_scalar_prefetch=1,
            grid=(cells // tile,),
            in_specs=[
                pl.BlockSpec((tile, half), lambda j, c: (j, 0)),
                pl.BlockSpec(memory_space=pl.ANY),
            ],
            out_specs=pl.BlockSpec((tile, half), lambda j, c: (j, 1 - c[0])),
        ),
        out_shape=jax.ShapeDtypeStruct(whole.shape, jnp.float32),
        input_output_aliases={2: 0},
        name="paste",
        cost_estimate=LIGHT,
    )(core, arrived, whole)


def on_device(footprint, flux, obs_weight, obs_count):
    _, lags, slots, cells = footprint.shape
    half = flux.shape[2] // 2
    rows = slots // CHUNKS
    chunks = range(CHUNKS)
    devices = lax.axis_size("tm")
    place = jnp.stack(
        [lax.axis_index("core"), lax.axis_index("tm"), jnp.int32(devices)]
    ).astype(jnp.int32)
    valid = (jnp.arange(slots, dtype=jnp.int32) < obs_count[0]).astype(jnp.float32)
    row_scale = (valid * obs_weight[0])[:, None]
    later = range(1, lags)
    paired = devices == lags and cells == half

    own, terms, weighted = [], [], []
    specs = [pl.BlockSpec((rows, cells), lambda j: (0, 0))] * len(later)
    other_specs = [pl.BlockSpec((rows, cells), lambda j, i=i: (i, 0)) for i in range(len(later))]

    def row_block(r, lag):
        return lambda tile: pl.BlockSpec((1, 1, rows, tile), lambda j, c: (0, lag, r, j))

    def column(r):
        return lambda tile: pl.BlockSpec((rows, tile), lambda j, c: (r, j))

    def payload(k):
        h, p, w = k, k - 2, k - 4
        up = terms[p] if 0 <= p < CHUNKS else []
        if h < CHUNKS:
            if up and paired:
                down, down_specs = [footprint] * len(later), [row_block(h, lag) for lag in later]
            else:
                down = cut(footprint, later, rows, h)
        elif w >= 0:
            value = weighted[w]
            if w > 1:
                value, done[0] = together(value, done[0])
            down, down_specs = [value] * len(later), [column(0)] * len(later)
        else:
            down = []
        if down and up and paired:
            return "one", choose(place, down, down_specs, up[::-1])
        return ("down" if not up else "both" if down else "up"), [*down, *up]

    def exchange(kind, sent):
        lags_of = {"down": [-1], "up": [1], "both": [-1, 1]}.get(kind)
        if kind == "one":
            return [cycled(value, lag) for value, lag in zip(sent, later)]
        ways = [way * lag for way in lags_of for lag in later]
        return [shifted(value, by) for value, by in zip(sent, ways)]

    def sorted_out(kind, arrived):
        count = len(later)
        if kind == "one":
            return arrived, arrived[::-1]
        low = arrived[:count] if kind != "up" else None
        return low, arrived[-count:] if kind != "down" else None

    def my_side(r, before):
        return [footprint, *own[r]], [row_block(r, 0)] + [column(0)] * len(later), before, 2 * half, True

    def their_side(r, before):
        foot = [foot_other] + [other[r]] * len(later)
        return foot, [column(r)] + [column(i) for i in range(len(later))], before, half, False

    other, done = [], [None, None]
    kind, sent = payload(0)
    for k in range(CHUNKS + 4):
        h, p, w = k, k - 2, k - 4
        if k == 0:
            flux, sent[0] = together(flux, sent[0])
        arrived, sort = exchange(kind, sent), kind
        if k == 1:
            arrived[0], same[0] = together(arrived[0], same[0])
        if k + 1 < CHUNKS + 4:
            kind, sent = payload(k + 1)
            for i in range(min(len(sent), len(arrived))):
                arrived[i], sent[i] = together(arrived[i], sent[i])
        low, high = sorted_out(sort, arrived)
        if k == 0:
            flux_parts = split(flux, swapped(side_of(flux, place)), place)
            foot_other = swapped(cut(footprint, [0], slots, 0)[0])
            same = forward(
                [footprint] * CHUNKS,
                [pl.BlockSpec((1, 1, rows, cells), lambda j, r=r: (0, 0, r, 0)) for r in chunks],
                [foot_other] * CHUNKS,
                [pl.BlockSpec((rows, cells), lambda j, r=r: (r, 0)) for r in chunks],
                rows, flux_parts,
            )
        if h < CHUNKS:
            own.append(low)
            other.append(swapped(stack(low)))
            terms.append(forward(low, specs, [other[h]] * len(later), other_specs, rows, flux_parts))
        if 0 <= p < CHUNKS:
            total = combine(row_scale, same[p], high, p, place)
            if p > 0:
                total, weighted[p - 1] = together(total, weighted[p - 1])
            weighted.append(lax.psum(total, "z"))
        if w >= 0:
            here = [weighted[w], *low]
            if w + 1 < CHUNKS:
                done[:] = adjoint(here, [my_side(w, done[0]), their_side(w, done[1])], place, cells)
    (theirs,) = adjoint(here, [their_side(w, done[1])], place, cells)
    (mine,) = adjoint(here, [my_side(w, done[0])], place, cells)
    return paste(swapped(theirs), mine, place)[None]


def solution(mesh):
    devices = mesh.devices
    split = Mesh(devices.reshape(devices.shape[0], devices.shape[1] // 2, 2), ("tm", "z", "core"))
    cells = ("z", "core")
    placed = (P("tm", None, None, cells), P("tm", cells, None), P("tm", None), P("tm"))
    return jax.shard_map(
        on_device, mesh=split, in_specs=placed, out_specs=P("tm", cells, None), check_vma=False
    )
```

```python
import functools

import jax
import jax.numpy as jnp
from jax import lax
from jax.experimental import pallas as pl
from jax.experimental.pallas import tpu as pltpu
from jax.sharding import Mesh, PartitionSpec as P

CHUNKS = 4
TILE = 256
WIDE = 512
LIGHT = pl.CostEstimate(flops=1, bytes_accessed=1, transcendentals=0)
IN_PLACE = pl.BlockSpec(memory_space=pl.ANY)
VMEM_LIMIT = 60 * 1024 * 1024


def shifted(value, by):
    devices = lax.axis_size("tm")
    pairs = [(i, i + by) for i in range(devices) if 0 <= i + by < devices]
    return lax.ppermute(value, "tm", pairs)


def cycled(value, by):
    devices = lax.axis_size("tm")
    return lax.ppermute(value, "tm", [(i, (i - by) % devices) for i in range(devices)])


def swapped(value):
    return lax.ppermute(value, "core", [(0, 1), (1, 0)])


def together(first, second):
    return lax.optimization_barrier((first, second))


def halves(value):
    high = value.astype(jnp.bfloat16)
    low = (value - high.astype(jnp.float32)).astype(jnp.bfloat16)
    return high, low


def times(left, right, dims):
    return lax.dot_general(left, right, (dims, ((), ())), preferred_element_type=jnp.float32)


def split_kernel(core_ref, own, other, high_ref, low_ref):
    cells = other.shape[0]
    for at, value in ((0, own[0]), (cells, other[...])):
        high, low = halves(value)
        high_ref[pl.ds(at, cells), :] = high
        low_ref[pl.ds(at, cells), :] = low


def split(flux, flux_other, core):
    cells, half = flux_other.shape
    tile = min(TILE, half)
    steps = half // tile
    block = pl.BlockSpec((2 * cells, tile), lambda j, c: (0, j))
    return list(pl.pallas_call(
        split_kernel,
        grid_spec=pltpu.PrefetchScalarGridSpec(
            num_scalar_prefetch=1,
            grid=(steps,),
            in_specs=[
                pl.BlockSpec((1, cells, tile), lambda j, c: (0, 0, c[0] * steps + j)),
                pl.BlockSpec((cells, tile), lambda j, c: (0, j)),
            ],
            out_specs=[block, block],
        ),
        out_shape=[jax.ShapeDtypeStruct((2 * cells, half), jnp.bfloat16)] * 2,
        name="split",
        cost_estimate=LIGHT,
    )(core, flux, flux_other))


def forward_kernel(count, *refs):
    foot_own, foot_other = refs[:count], refs[count:2 * count]
    flux_high, flux_low = refs[2 * count:2 * count + 2]
    outs = refs[2 * count + 2:3 * count + 2]
    parts_ref = refs[-1]
    rows, cells = foot_own[0].shape[-2:]
    depth = count * rows

    @pl.when(pl.program_id(0) == 0)
    def _():
        for i in range(count):
            for side, source in ((0, foot_own[i]), (1, foot_other[i])):
                high, low = halves(source[...].reshape(rows, cells))
                columns = pl.ds(side * cells, cells)
                parts_ref[pl.ds(i * rows, rows), columns] = high
                parts_ref[pl.ds(depth + i * rows, rows), columns] = low

    dims = ((1,), (0,))
    both = times(parts_ref[...], flux_high[...], dims)
    total = both[:depth] + both[depth:] + times(parts_ref[pl.ds(0, depth), :], flux_low[...], dims)
    for i in range(count):
        outs[i][...] = total[i * rows:(i + 1) * rows]


def forward(foot_own, own_specs, foot_other, other_specs, rows, flux_parts):
    count = len(foot_own)
    depth, half = flux_parts[0].shape
    tile = min(WIDE, half)
    outs = pl.pallas_call(
        functools.partial(forward_kernel, count),
        grid=(half // tile,),
        in_specs=[
            *own_specs,
            *other_specs,
            *[pl.BlockSpec((depth, tile), lambda j: (0, j))] * 2,
        ],
        out_specs=[pl.BlockSpec((rows, tile), lambda j: (0, j))] * count,
        scratch_shapes=[pltpu.VMEM((2 * count * rows, depth), jnp.bfloat16)],
        out_shape=[jax.ShapeDtypeStruct((rows, half), jnp.float32)] * count,
        compiler_params=pltpu.CompilerParams(vmem_limit_bytes=VMEM_LIMIT),
        name="forward",
        cost_estimate=LIGHT,
    )(*foot_own, *foot_other, *flux_parts)
    return list(outs)


def adjoint_kernel(count, sides, first, place_ref, *refs):
    weighted, refs = refs[:count], refs[count:]
    foot, refs = refs[:sides * count], refs[sides * count:]
    before, refs = (None, refs) if first else (refs[:sides], refs[sides:])
    outs, (high_ref, low_ref) = refs[:sides], refs[sides:]
    rows, tile = foot[0].shape[-2:]

    @pl.when(pl.program_id(0) == 0)
    def _():
        for i in range(count):
            value = jnp.where(place_ref[1] + i < place_ref[2], weighted[i][...], 0.0)
            high, low = halves(value)
            high_ref[pl.ds(i * rows, rows), :] = high
            low_ref[pl.ds(i * rows, rows), :] = low

    dims = ((1,), (0,))
    for side in range(sides):
        mine = foot[side * count:(side + 1) * count]
        slab = jnp.concatenate([ref[...].reshape(rows, tile) for ref in mine], axis=0)
        high, low = halves(slab.T)
        both = times(jnp.concatenate([high, low], axis=0), high_ref[...], dims)
        total = both[:tile] + both[tile:] + times(high, low_ref[...], dims)
        if not first:
            total = total + before[side][...]
        outs[side][...] = total


def adjoint(weighted, sides, core, cells):
    count = len(weighted)
    rows, half = weighted[0].shape
    tile = min(WIDE, cells)
    first = sides[0][2] is None
    out_specs = []
    for side in sides:
        if side[4]:
            out_specs.append(pl.BlockSpec((tile, half), lambda j, c: (j, c[0])))
        else:
            out_specs.append(pl.BlockSpec((tile, half), lambda j, c: (j, 0)))
    foot = [array for side in sides for array in side[0]]
    earlier = [] if first else [side[2] for side in sides]
    at = 1 + count + len(foot)
    return pl.pallas_call(
        functools.partial(adjoint_kernel, count, len(sides), first),
        grid_spec=pltpu.PrefetchScalarGridSpec(
            num_scalar_prefetch=1,
            grid=(cells // tile,),
            in_specs=[
                *[pl.BlockSpec((rows, half), lambda j, c: (0, 0))] * count,
                *[spec(tile) for side in sides for spec in side[1]],
                *([] if first else out_specs),
            ],
            out_specs=out_specs,
            scratch_shapes=[pltpu.VMEM((count * rows, half), jnp.bfloat16)] * 2,
        ),
        out_shape=[jax.ShapeDtypeStruct((cells, side[3]), jnp.float32) for side in sides],
        input_output_aliases={} if first else {at + i: i for i in range(len(sides))},
        compiler_params=pltpu.CompilerParams(vmem_limit_bytes=VMEM_LIMIT),
        name="adjoint",
        cost_estimate=LIGHT,
    )(core, *weighted, *foot, *earlier)


def run(copies):
    for copy in copies:
        copy.start()
    for copy in copies:
        copy.wait()


def cut_kernel(lags, r, footprint, *refs):
    outs, sems = refs[:-1], refs[-1]
    rows = outs[0].shape[0]
    run([
        pltpu.make_async_copy(footprint.at[0, lag, pl.ds(r * rows, rows), :], out, sems.at[i])
        for i, (lag, out) in enumerate(zip(lags, outs))
    ])


def cut(footprint, lags, rows, r):
    return list(pl.pallas_call(
        functools.partial(cut_kernel, lags, r),
        in_specs=[IN_PLACE],
        out_specs=[IN_PLACE] * len(lags),
        scratch_shapes=[pltpu.SemaphoreType.DMA((len(lags),))],
        out_shape=[jax.ShapeDtypeStruct((rows, footprint.shape[3]), jnp.float32)] * len(lags),
        name="cut",
        cost_estimate=LIGHT,
    )(footprint))


def stack_kernel(*refs):
    pieces, out, sems = refs[:-2], refs[-2], refs[-1]
    rows = pieces[0].shape[0]
    run([
        pltpu.make_async_copy(piece, out.at[pl.ds(i * rows, rows), :], sems.at[i])
        for i, piece in enumerate(pieces)
    ])


def stack(pieces):
    rows, cells = pieces[0].shape
    return pl.pallas_call(
        stack_kernel,
        in_specs=[IN_PLACE] * len(pieces),
        out_specs=IN_PLACE,
        scratch_shapes=[pltpu.SemaphoreType.DMA((len(pieces),))],
        out_shape=jax.ShapeDtypeStruct((rows * len(pieces), cells), jnp.float32),
        name="stack",
        cost_estimate=LIGHT,
    )(*pieces)


def side_kernel(core_ref, flux, out):
    out[...] = flux[0]


def side_of(flux, core):
    _, cells, width = flux.shape
    tile = min(TILE, width // 2)
    steps = width // 2 // tile
    return pl.pallas_call(
        side_kernel,
        grid_spec=pltpu.PrefetchScalarGridSpec(
            num_scalar_prefetch=1,
            grid=(steps,),
            in_specs=[pl.BlockSpec((1, cells, tile), lambda j, c: (0, 0, (1 - c[0]) * steps + j))],
            out_specs=pl.BlockSpec((cells, tile), lambda j, c: (0, j)),
        ),
        out_shape=jax.ShapeDtypeStruct((cells, width // 2), jnp.float32),
        name="side",
        cost_estimate=LIGHT,
    )(core, flux)


def combine_kernel(place_ref, scale, same, *refs):
    total = same[...]
    for lag, ref in enumerate(refs[:-1], 1):
        total = total + jnp.where(place_ref[1] >= lag, ref[...], 0.0)
    refs[-1][...] = scale[...] * total


def combine(scale, same, arrived, r, place):
    rows, half = same.shape
    tile = min(WIDE, half)
    block = pl.BlockSpec((rows, tile), lambda j, c: (0, j))
    return pl.pallas_call(
        combine_kernel,
        grid_spec=pltpu.PrefetchScalarGridSpec(
            num_scalar_prefetch=1,
            grid=(half // tile,),
            in_specs=[
                pl.BlockSpec((rows, 1), lambda j, c: (r, 0)),
                block,
                *[block] * len(arrived),
            ],
            out_specs=block,
        ),
        out_shape=jax.ShapeDtypeStruct((rows, half), jnp.float32),
        name="combine",
        cost_estimate=LIGHT,
    )(place, scale, same, *arrived)


def choose_kernel(r, place_ref, source, *refs):
    count = len(refs) // 2
    ups, outs, sems = refs[:count], refs[count:2 * count], refs[-1]
    rows = outs[0].shape[0]
    choices = []
    for i, (up, out) in enumerate(zip(ups, outs)):
        down = source if r is None else source.at[0, i + 1, pl.ds(r * rows, rows), :]
        below = place_ref[1] > i
        choices.append((below, pltpu.make_async_copy(down, out, sems.at[i])))
        choices.append((jnp.logical_not(below), pltpu.make_async_copy(up, out, sems.at[i])))
    for taken, copy in choices:
        pl.when(taken)(copy.start)
    for taken, copy in choices:
        pl.when(taken)(copy.wait)


def choose(place, source, r, up):
    rows, width = up[0].shape
    return list(pl.pallas_call(
        functools.partial(choose_kernel, r),
        in_specs=[pl.BlockSpec(memory_space=pltpu.SMEM)] + [IN_PLACE] * (1 + len(up)),
        out_specs=[IN_PLACE] * len(up),
        scratch_shapes=[pltpu.SemaphoreType.DMA((len(up),))],
        out_shape=[jax.ShapeDtypeStruct((rows, width), jnp.float32)] * len(up),
        name="choose",
        cost_estimate=LIGHT,
    )(place, source, *up))


def paste_kernel(parts, place_ref, arrived, before, out, sems):
    cells, half = arrived.shape
    rows = cells // parts
    left = pl.multiple_of((1 - place_ref[0]) * half, 128)
    copies = []
    for i in range(parts):
        at = pl.ds(i * rows, rows)
        copies.append(pltpu.make_async_copy(
            arrived.at[at, :], out.at[at, pl.ds(left, half)], sems.at[i]
        ))
    run(copies)


def paste(arrived, whole, place):
    parts = 4
    return pl.pallas_call(
        functools.partial(paste_kernel, parts),
        in_specs=[
            pl.BlockSpec(memory_space=pltpu.SMEM),
            IN_PLACE,
            IN_PLACE,
        ],
        out_specs=IN_PLACE,
        scratch_shapes=[pltpu.SemaphoreType.DMA((parts,))],
        out_shape=jax.ShapeDtypeStruct(whole.shape, jnp.float32),
        input_output_aliases={2: 0},
        name="paste",
        cost_estimate=LIGHT,
    )(place, arrived, whole)


def on_device(footprint, flux, obs_weight, obs_count):
    _, lags, slots, cells = footprint.shape
    half = flux.shape[2] // 2
    rows = slots // CHUNKS
    chunks = range(CHUNKS)
    devices = lax.axis_size("tm")
    place = jnp.stack(
        [lax.axis_index("core"), lax.axis_index("tm"), jnp.int32(devices)]
    ).astype(jnp.int32)
    valid = (jnp.arange(slots, dtype=jnp.int32) < obs_count[0]).astype(jnp.float32)
    row_scale = (valid * obs_weight[0])[:, None]
    later = range(1, lags)
    paired = devices == lags and cells == half

    own, terms, weighted = [], [], []
    specs = [pl.BlockSpec((rows, cells), lambda j: (0, 0))] * len(later)
    other_specs = [pl.BlockSpec((rows, cells), lambda j, i=i: (i, 0)) for i in range(len(later))]

    def row_block(r, lag):
        return lambda tile: pl.BlockSpec((1, 1, rows, tile), lambda j, c: (0, lag, r, j))

    def column(r):
        return lambda tile: pl.BlockSpec((rows, tile), lambda j, c: (r, j))

    def payload(k):
        h, p, w = k, k - 2, k - 4
        up = terms[p] if 0 <= p < CHUNKS else []
        down = []
        if h < CHUNKS:
            if up and paired:
                return "one", choose(place, footprint, h, up[::-1])
            down = cut(footprint, later, rows, h)
        elif w >= 0:
            value = weighted[w]
            if w > 1:
                value, done[0] = together(value, done[0])
            if up and paired:
                return "one", choose(place, value, None, up[::-1])
            down = [value] * len(later)
        return ("down" if not up else "both" if down else "up"), [*down, *up]

    def exchange(kind, sent):
        lags_of = {"down": [-1], "up": [1], "both": [-1, 1]}.get(kind)
        if kind == "one":
            return [cycled(value, lag) for value, lag in zip(sent, later)]
        ways = [way * lag for way in lags_of for lag in later]
        return [shifted(value, by) for value, by in zip(sent, ways)]

    def sorted_out(kind, arrived):
        count = len(later)
        if kind == "one":
            return arrived, arrived[::-1]
        low = arrived[:count] if kind != "up" else None
        return low, arrived[-count:] if kind != "down" else None

    def my_side(r, before):
        return [footprint, *own[r]], [row_block(r, 0)] + [column(0)] * len(later), before, 2 * half, True

    def their_side(r, before):
        foot = [foot_other] + [other[r]] * len(later)
        return foot, [column(r)] + [column(i) for i in range(len(later))], before, half, False

    other, done = [], [None, None]
    kind, sent = payload(0)
    flux, sent[0] = together(flux, sent[0])
    flux_parts = split(flux, swapped(side_of(flux, place)), place)
    foot_other = swapped(cut(footprint, [0], slots, 0)[0])
    same = forward(
        [footprint] * CHUNKS,
        [pl.BlockSpec((1, 1, rows, cells), lambda j, r=r: (0, 0, r, 0)) for r in chunks],
        [foot_other] * CHUNKS,
        [pl.BlockSpec((rows, cells), lambda j, r=r: (r, 0)) for r in chunks],
        rows, flux_parts,
    )
    for k in range(CHUNKS + 4):
        h, p, w = k, k - 2, k - 4
        arrived, sort = exchange(kind, sent), kind
        if k == 0:
            arrived[0], flux_parts[0] = together(arrived[0], flux_parts[0])
        if k == 2:
            arrived[0], same[0] = together(arrived[0], same[0])
        if k + 1 < CHUNKS + 4:
            kind, sent = payload(k + 1)
            for i in range(min(len(sent), len(arrived))):
                arrived[i], sent[i] = together(arrived[i], sent[i])
        low, high = sorted_out(sort, arrived)
        if h < CHUNKS:
            own.append(low)
            other.append(swapped(stack(low)))
            terms.append(forward(low, specs, [other[h]] * len(later), other_specs, rows, flux_parts))
        if 0 <= p < CHUNKS:
            total = combine(row_scale, same[p], high, p, place)
            if p > 0:
                total, weighted[p - 1] = together(total, weighted[p - 1])
            weighted.append(lax.psum(total, "z"))
        if w >= 0:
            here = [weighted[w], *low]
            if w + 1 < CHUNKS:
                done[:] = adjoint(here, [my_side(w, done[0]), their_side(w, done[1])], place, cells)
    (theirs,) = adjoint(here, [their_side(w, done[1])], place, cells)
    (mine,) = adjoint(here, [my_side(w, done[0])], place, cells)
    return paste(swapped(theirs), mine, place)[None]


def solution(mesh):
    devices = mesh.devices
    split = Mesh(devices.reshape(devices.shape[0], devices.shape[1] // 2, 2), ("tm", "z", "core"))
    cells = ("z", "core")
    placed = (P("tm", None, None, cells), P("tm", cells, None), P("tm", None), P("tm"))
    return jax.shard_map(
        on_device, mesh=split, in_specs=placed, out_specs=P("tm", cells, None), check_vma=False
    )
```

```python
import functools

import jax
import jax.numpy as jnp
from jax import lax
from jax.experimental import pallas as pl
from jax.experimental.pallas import tpu as pltpu
from jax.sharding import Mesh, PartitionSpec as P

CHUNKS = 4
PARTS = 8
TILE = 256
WIDE = 512
LIGHT = pl.CostEstimate(flops=1, bytes_accessed=1, transcendentals=0)
IN_PLACE = pl.BlockSpec(memory_space=pl.ANY)
VMEM_LIMIT = 60 * 1024 * 1024


def shifted(value, by):
    devices = lax.axis_size("tm")
    pairs = [(i, i + by) for i in range(devices) if 0 <= i + by < devices]
    return lax.ppermute(value, "tm", pairs)


def cycled(value, by):
    devices = lax.axis_size("tm")
    return lax.ppermute(value, "tm", [(i, (i - by) % devices) for i in range(devices)])


def swapped(value):
    return lax.ppermute(value, "core", [(0, 1), (1, 0)])


def together(first, second):
    return lax.optimization_barrier((first, second))


def halves(value):
    high = value.astype(jnp.bfloat16)
    low = (value - high.astype(jnp.float32)).astype(jnp.bfloat16)
    return high, low


def times(left, right, dims):
    return lax.dot_general(left, right, (dims, ((), ())), preferred_element_type=jnp.float32)


def split_kernel(core_ref, own, other, out):
    cells = other.shape[0]
    for at, value in ((0, own[0]), (cells, other[...])):
        high, low = halves(value)
        for block, part in enumerate((high, high, low)):
            out[pl.ds(block * 2 * cells + at, cells), :] = part


def split(flux, flux_other, core):
    cells, half = flux_other.shape
    tile = min(TILE, half)
    steps = half // tile
    return pl.pallas_call(
        split_kernel,
        grid_spec=pltpu.PrefetchScalarGridSpec(
            num_scalar_prefetch=1,
            grid=(steps,),
            in_specs=[
                pl.BlockSpec((1, cells, tile), lambda j, c: (0, 0, c[0] * steps + j)),
                pl.BlockSpec((cells, tile), lambda j, c: (0, j)),
            ],
            out_specs=pl.BlockSpec((6 * cells, tile), lambda j, c: (0, j)),
        ),
        out_shape=jax.ShapeDtypeStruct((6 * cells, half), jnp.bfloat16),
        compiler_params=pltpu.CompilerParams(vmem_limit_bytes=VMEM_LIMIT),
        name="split",
        cost_estimate=LIGHT,
    )(core, flux, flux_other)


def forward_kernel(count, *refs):
    foot_own, foot_other = refs[:count], refs[count:2 * count]
    flux_parts, outs, parts_ref = refs[2 * count], refs[2 * count + 1:-1], refs[-1]
    rows, cells = foot_own[0].shape[-2:]

    @pl.when(pl.program_id(0) == 0)
    def _():
        for i in range(count):
            for side, source in ((0, foot_own[i]), (1, foot_other[i])):
                high, low = halves(source[...].reshape(rows, cells))
                for block, part in enumerate((high, low, high)):
                    columns = pl.ds((2 * block + side) * cells, cells)
                    parts_ref[pl.ds(i * rows, rows), columns] = part

    total = times(parts_ref[...], flux_parts[...], ((1,), (0,)))
    for i in range(count):
        outs[i][...] = total[i * rows:(i + 1) * rows]


def forward(foot_own, own_specs, foot_other, other_specs, rows, flux_parts):
    count = len(foot_own)
    depth, half = flux_parts.shape
    tile = min(TILE, half)
    outs = pl.pallas_call(
        functools.partial(forward_kernel, count),
        grid=(half // tile,),
        in_specs=[
            *own_specs,
            *other_specs,
            pl.BlockSpec((depth, tile), lambda j: (0, j)),
        ],
        out_specs=[pl.BlockSpec((rows, tile), lambda j: (0, j))] * count,
        scratch_shapes=[pltpu.VMEM((count * rows, depth), jnp.bfloat16)],
        out_shape=[jax.ShapeDtypeStruct((rows, half), jnp.float32)] * count,
        compiler_params=pltpu.CompilerParams(vmem_limit_bytes=VMEM_LIMIT),
        name="forward",
        cost_estimate=LIGHT,
    )(*foot_own, *foot_other, flux_parts)
    return list(outs)


def adjoint_kernel(count, sides, first, place_ref, *refs):
    weighted, refs = refs[:count], refs[count:]
    foot, refs = refs[:sides * count], refs[sides * count:]
    before, refs = (None, refs) if first else (refs[:sides], refs[sides:])
    outs, parts_ref = refs[:sides], refs[sides]
    rows, tile = foot[0].shape[-2:]
    depth = count * rows

    @pl.when(pl.program_id(0) == 0)
    def _():
        for i in range(count):
            value = jnp.where(place_ref[1] + i < place_ref[2], weighted[i][...], 0.0)
            high, low = halves(value)
            for block, part in enumerate((high, high, low)):
                parts_ref[pl.ds(block * depth + i * rows, rows), :] = part

    for side in range(sides):
        mine = foot[side * count:(side + 1) * count]
        slab = jnp.concatenate([ref[...].reshape(rows, tile) for ref in mine], axis=0)
        high, low = halves(slab.T)
        total = times(jnp.concatenate([high, low, high], axis=1), parts_ref[...], ((1,), (0,)))
        if not first:
            total = total + before[side][...]
        outs[side][...] = total


def adjoint(weighted, sides, core, cells):
    count = len(weighted)
    rows, half = weighted[0].shape
    tile = min(WIDE, cells)
    first = sides[0][2] is None
    out_specs = []
    for side in sides:
        if side[4]:
            out_specs.append(pl.BlockSpec((tile, half), lambda j, c: (j, c[0])))
        else:
            out_specs.append(pl.BlockSpec((tile, half), lambda j, c: (j, 0)))
    foot = [array for side in sides for array in side[0]]
    earlier = [] if first else [side[2] for side in sides]
    at = 1 + count + len(foot)
    return pl.pallas_call(
        functools.partial(adjoint_kernel, count, len(sides), first),
        grid_spec=pltpu.PrefetchScalarGridSpec(
            num_scalar_prefetch=1,
            grid=(cells // tile,),
            in_specs=[
                *[pl.BlockSpec((rows, half), lambda j, c: (0, 0))] * count,
                *[spec(tile) for side in sides for spec in side[1]],
                *([] if first else out_specs),
            ],
            out_specs=out_specs,
            scratch_shapes=[pltpu.VMEM((3 * count * rows, half), jnp.bfloat16)],
        ),
        out_shape=[jax.ShapeDtypeStruct((cells, side[3]), jnp.float32) for side in sides],
        input_output_aliases={} if first else {at + i: i for i in range(len(sides))},
        compiler_params=pltpu.CompilerParams(vmem_limit_bytes=VMEM_LIMIT),
        name="adjoint",
        cost_estimate=LIGHT,
    )(core, *weighted, *foot, *earlier)


def through(buffer, sems, moves):
    loads = [pltpu.make_async_copy(a, buffer.at[i], sems.at[0, i]) for i, (a, _) in enumerate(moves)]
    stores = [pltpu.make_async_copy(buffer.at[i], b, sems.at[1, i]) for i, (_, b) in enumerate(moves)]
    for load in loads:
        load.start()
    for load, store in zip(loads, stores):
        load.wait()
        store.start()
    for store in stores:
        store.wait()


def passage(count, rows, columns):
    return [pltpu.VMEM((count, rows, columns), jnp.float32), pltpu.SemaphoreType.DMA((2, count))]


def cut_kernel(lags, r, footprint, *refs):
    outs, buffer, sems = refs[:-2], refs[-2], refs[-1]
    rows = outs[0].shape[0]
    through(buffer, sems, [
        (footprint.at[0, lag, pl.ds(r * rows, rows), :], out) for lag, out in zip(lags, outs)
    ])


def cut(footprint, lags, rows, r):
    return list(pl.pallas_call(
        functools.partial(cut_kernel, lags, r),
        in_specs=[IN_PLACE],
        out_specs=[IN_PLACE] * len(lags),
        scratch_shapes=passage(len(lags), rows, footprint.shape[3]),
        out_shape=[jax.ShapeDtypeStruct((rows, footprint.shape[3]), jnp.float32)] * len(lags),
        name="cut",
        cost_estimate=LIGHT,
    )(footprint))


def stack_kernel(*refs):
    pieces, out, buffer, sems = refs[:-3], refs[-3], refs[-2], refs[-1]
    rows = pieces[0].shape[0]
    through(buffer, sems, [(piece, out.at[pl.ds(i * rows, rows), :]) for i, piece in enumerate(pieces)])


def stack(pieces):
    rows, cells = pieces[0].shape
    return pl.pallas_call(
        stack_kernel,
        in_specs=[IN_PLACE] * len(pieces),
        out_specs=IN_PLACE,
        scratch_shapes=passage(len(pieces), rows, cells),
        out_shape=jax.ShapeDtypeStruct((rows * len(pieces), cells), jnp.float32),
        name="stack",
        cost_estimate=LIGHT,
    )(*pieces)


def side_kernel(parts, place_ref, flux, out, buffer, sems):
    cells, half = out.shape
    rows = cells // parts
    left = pl.multiple_of((1 - place_ref[0]) * half, 128)
    bands = [pl.ds(i * rows, rows) for i in range(parts)]
    through(buffer, sems, [(flux.at[0, at, pl.ds(left, half)], out.at[at, :]) for at in bands])


def side_of(flux, place):
    _, cells, width = flux.shape
    return pl.pallas_call(
        functools.partial(side_kernel, PARTS),
        in_specs=[pl.BlockSpec(memory_space=pltpu.SMEM), IN_PLACE],
        out_specs=IN_PLACE,
        scratch_shapes=passage(PARTS, cells // PARTS, width // 2),
        out_shape=jax.ShapeDtypeStruct((cells, width // 2), jnp.float32),
        name="side",
        cost_estimate=LIGHT,
    )(place, flux)


def combine_kernel(place_ref, scale, same, *refs):
    total = same[...]
    for lag, ref in enumerate(refs[:-1], 1):
        total = total + jnp.where(place_ref[1] >= lag, ref[...], 0.0)
    refs[-1][...] = scale[...] * total


def combine(scale, same, arrived, r, place):
    rows, half = same.shape
    tile = min(WIDE, half)
    block = pl.BlockSpec((rows, tile), lambda j, c: (0, j))
    return pl.pallas_call(
        combine_kernel,
        grid_spec=pltpu.PrefetchScalarGridSpec(
            num_scalar_prefetch=1,
            grid=(half // tile,),
            in_specs=[
                pl.BlockSpec((rows, 1), lambda j, c: (r, 0)),
                block,
                *[block] * len(arrived),
            ],
            out_specs=block,
        ),
        out_shape=jax.ShapeDtypeStruct((rows, half), jnp.float32),
        name="combine",
        cost_estimate=LIGHT,
    )(place, scale, same, *arrived)


def choose_kernel(r, place_ref, source, *refs):
    count = len(refs) // 2 - 1
    ups, outs, buffer, sems = refs[:count], refs[count:2 * count], refs[-2], refs[-1]
    rows = outs[0].shape[0]
    loads, stores = [], []
    for i, (up, out) in enumerate(zip(ups, outs)):
        down = source if r is None else source.at[0, i + 1, pl.ds(r * rows, rows), :]
        below = place_ref[1] > i
        loads.append([
            (below, pltpu.make_async_copy(down, buffer.at[i], sems.at[0, i])),
            (jnp.logical_not(below), pltpu.make_async_copy(up, buffer.at[i], sems.at[0, i])),
        ])
        stores.append(pltpu.make_async_copy(buffer.at[i], out, sems.at[1, i]))
    for pair in loads:
        for taken, load in pair:
            pl.when(taken)(load.start)
    for pair, store in zip(loads, stores):
        for taken, load in pair:
            pl.when(taken)(load.wait)
        store.start()
    for store in stores:
        store.wait()


def choose(place, source, r, up):
    rows, width = up[0].shape
    return list(pl.pallas_call(
        functools.partial(choose_kernel, r),
        in_specs=[pl.BlockSpec(memory_space=pltpu.SMEM)] + [IN_PLACE] * (1 + len(up)),
        out_specs=[IN_PLACE] * len(up),
        scratch_shapes=passage(len(up), rows, width),
        out_shape=[jax.ShapeDtypeStruct((rows, width), jnp.float32)] * len(up),
        name="choose",
        cost_estimate=LIGHT,
    )(place, source, *up))


def paste_kernel(parts, place_ref, arrived, before, out, buffer, sems):
    cells, half = arrived.shape
    rows = cells // parts
    left = pl.multiple_of((1 - place_ref[0]) * half, 128)
    bands = [pl.ds(i * rows, rows) for i in range(parts)]
    through(buffer, sems, [(arrived.at[at, :], out.at[at, pl.ds(left, half)]) for at in bands])


def paste(arrived, whole, place):
    cells, half = arrived.shape
    return pl.pallas_call(
        functools.partial(paste_kernel, PARTS),
        in_specs=[pl.BlockSpec(memory_space=pltpu.SMEM), IN_PLACE, IN_PLACE],
        out_specs=IN_PLACE,
        scratch_shapes=passage(PARTS, cells // PARTS, half),
        out_shape=jax.ShapeDtypeStruct(whole.shape, jnp.float32),
        input_output_aliases={2: 0},
        name="paste",
        cost_estimate=LIGHT,
    )(place, arrived, whole)


def on_device(footprint, flux, obs_weight, obs_count):
    _, lags, slots, cells = footprint.shape
    half = flux.shape[2] // 2
    rows = slots // CHUNKS
    chunks = range(CHUNKS)
    devices = lax.axis_size("tm")
    place = jnp.stack(
        [lax.axis_index("core"), lax.axis_index("tm"), jnp.int32(devices)]
    ).astype(jnp.int32)
    valid = (jnp.arange(slots, dtype=jnp.int32) < obs_count[0]).astype(jnp.float32)
    row_scale = (valid * obs_weight[0])[:, None]
    later = range(1, lags)
    paired = devices == lags and cells == half

    own, terms, weighted = [], [], []
    specs = [pl.BlockSpec((rows, cells), lambda j: (0, 0))] * len(later)
    other_specs = [pl.BlockSpec((rows, cells), lambda j, i=i: (i, 0)) for i in range(len(later))]

    def row_block(r, lag):
        return lambda tile: pl.BlockSpec((1, 1, rows, tile), lambda j, c: (0, lag, r, j))

    def column(r):
        return lambda tile: pl.BlockSpec((rows, tile), lambda j, c: (r, j))

    def payload(k):
        h, p, w = k, k - 2, k - 4
        up = terms[p] if 0 <= p < CHUNKS else []
        down = []
        if h < CHUNKS:
            if up and paired:
                return "one", choose(place, footprint, h, up[::-1])
            down = cut(footprint, later, rows, h)
        elif w >= 0:
            value = weighted[w]
            if w > 1:
                value, done[0] = together(value, done[0])
            if up and paired:
                return "one", choose(place, value, None, up[::-1])
            down = [value] * len(later)
        return ("down" if not up else "both" if down else "up"), [*down, *up]

    def exchange(kind, sent):
        lags_of = {"down": [-1], "up": [1], "both": [-1, 1]}.get(kind)
        if kind == "one":
            return [cycled(value, lag) for value, lag in zip(sent, later)]
        ways = [way * lag for way in lags_of for lag in later]
        return [shifted(value, by) for value, by in zip(sent, ways)]

    def sorted_out(kind, arrived):
        count = len(later)
        if kind == "one":
            return arrived, arrived[::-1]
        low = arrived[:count] if kind != "up" else None
        return low, arrived[-count:] if kind != "down" else None

    def my_side(r, before):
        return [footprint, *own[r]], [row_block(r, 0)] + [column(0)] * len(later), before, 2 * half, True

    def their_side(r, before):
        foot = [foot_other] + [other[r]] * len(later)
        return foot, [column(r)] + [column(i) for i in range(len(later))], before, half, False

    other, done = [], [None, None]
    kind, sent = payload(0)
    flux, sent[0] = together(flux, sent[0])
    flux_parts = split(flux, swapped(side_of(flux, place)), place)
    foot_other = swapped(cut(footprint, [0], slots, 0)[0])
    same = forward(
        [footprint] * CHUNKS,
        [pl.BlockSpec((1, 1, rows, cells), lambda j, r=r: (0, 0, r, 0)) for r in chunks],
        [foot_other] * CHUNKS,
        [pl.BlockSpec((rows, cells), lambda j, r=r: (r, 0)) for r in chunks],
        rows, flux_parts,
    )
    for k in range(CHUNKS + 4):
        h, p, w = k, k - 2, k - 4
        arrived, sort = exchange(kind, sent), kind
        if k == 0:
            arrived[0], flux_parts = together(arrived[0], flux_parts)
        if k == 2:
            arrived[0], same[0] = together(arrived[0], same[0])
        if k + 1 < CHUNKS + 4:
            kind, sent = payload(k + 1)
            for i in range(min(len(sent), len(arrived))):
                arrived[i], sent[i] = together(arrived[i], sent[i])
        low, high = sorted_out(sort, arrived)
        if h < CHUNKS:
            own.append(low)
            other.append(swapped(stack(low)))
            terms.append(forward(low, specs, [other[h]] * len(later), other_specs, rows, flux_parts))
        if 0 <= p < CHUNKS:
            total = combine(row_scale, same[p], high, p, place)
            if p > 0:
                total, weighted[p - 1] = together(total, weighted[p - 1])
            weighted.append(lax.psum(total, "z"))
        if w >= 0:
            here = [weighted[w], *low]
            if w + 1 < CHUNKS:
                done[:] = adjoint(here, [my_side(w, done[0]), their_side(w, done[1])], place, cells)
    (theirs,) = adjoint(here, [their_side(w, done[1])], place, cells)
    (mine,) = adjoint(here, [my_side(w, done[0])], place, cells)
    return paste(swapped(theirs), mine, place)[None]


def solution(mesh):
    devices = mesh.devices
    split = Mesh(devices.reshape(devices.shape[0], devices.shape[1] // 2, 2), ("tm", "z", "core"))
    cells = ("z", "core")
    placed = (P("tm", None, None, cells), P("tm", cells, None), P("tm", None), P("tm"))
    return jax.shard_map(
        on_device, mesh=split, in_specs=placed, out_specs=P("tm", cells, None), check_vma=False
    )
```

```python
import functools

import jax
import jax.numpy as jnp
from jax import lax
from jax.experimental import pallas as pl
from jax.experimental.pallas import tpu as pltpu
from jax.sharding import Mesh, PartitionSpec as P

CHUNKS = 4
PARTS = 8
TILE = 256
WIDE = 512
LIGHT = pl.CostEstimate(flops=1, bytes_accessed=1, transcendentals=0)
IN_PLACE = pl.BlockSpec(memory_space=pl.ANY)
VMEM_LIMIT = 60 * 1024 * 1024


def shifted(value, by):
    devices = lax.axis_size("tm")
    pairs = [(i, i + by) for i in range(devices) if 0 <= i + by < devices]
    return lax.ppermute(value, "tm", pairs)


def cycled(value, by):
    devices = lax.axis_size("tm")
    return lax.ppermute(value, "tm", [(i, (i - by) % devices) for i in range(devices)])


def swapped(value):
    return lax.ppermute(value, "core", [(0, 1), (1, 0)])


def together(first, second):
    return lax.optimization_barrier((first, second))


def halves(value):
    high = value.astype(jnp.bfloat16)
    low = (value - high.astype(jnp.float32)).astype(jnp.bfloat16)
    return high, low


def times(left, right, dims):
    return lax.dot_general(left, right, (dims, ((), ())), preferred_element_type=jnp.float32)


def split_kernel(core_ref, own, other, out):
    cells = other.shape[0]
    for at, value in ((0, own[0]), (cells, other[...])):
        high, low = halves(value)
        for block, part in enumerate((high, high, low)):
            out[pl.ds(block * 2 * cells + at, cells), :] = part


def split(flux, flux_other, core):
    cells, half = flux_other.shape
    tile = min(TILE, half)
    steps = half // tile
    return pl.pallas_call(
        split_kernel,
        grid_spec=pltpu.PrefetchScalarGridSpec(
            num_scalar_prefetch=1,
            grid=(steps,),
            in_specs=[
                pl.BlockSpec((1, cells, tile), lambda j, c: (0, 0, c[0] * steps + j)),
                pl.BlockSpec((cells, tile), lambda j, c: (0, j)),
            ],
            out_specs=pl.BlockSpec((6 * cells, tile), lambda j, c: (0, j)),
        ),
        out_shape=jax.ShapeDtypeStruct((6 * cells, half), jnp.bfloat16),
        compiler_params=pltpu.CompilerParams(vmem_limit_bytes=VMEM_LIMIT),
        name="split",
        cost_estimate=LIGHT,
    )(core, flux, flux_other)


def forward_kernel(count, *refs):
    foot_own, foot_other = refs[:count], refs[count:2 * count]
    flux_parts, outs, parts_ref = refs[2 * count], refs[2 * count + 1:-1], refs[-1]
    rows, cells = foot_own[0].shape[-2:]

    @pl.when(pl.program_id(0) == 0)
    def _():
        for i in range(count):
            for side, source in ((0, foot_own[i]), (1, foot_other[i])):
                high, low = halves(source[...].reshape(rows, cells))
                for block, part in enumerate((high, low, high)):
                    columns = pl.ds((2 * block + side) * cells, cells)
                    parts_ref[pl.ds(i * rows, rows), columns] = part

    total = times(parts_ref[...], flux_parts[...], ((1,), (0,)))
    for i in range(count):
        outs[i][...] = total[i * rows:(i + 1) * rows]


def forward(foot_own, own_specs, foot_other, other_specs, rows, flux_parts):
    count = len(foot_own)
    depth, half = flux_parts.shape
    tile = min(TILE, half)
    outs = pl.pallas_call(
        functools.partial(forward_kernel, count),
        grid=(half // tile,),
        in_specs=[
            *own_specs,
            *other_specs,
            pl.BlockSpec((depth, tile), lambda j: (0, j)),
        ],
        out_specs=[pl.BlockSpec((rows, tile), lambda j: (0, j))] * count,
        scratch_shapes=[pltpu.VMEM((count * rows, depth), jnp.bfloat16)],
        out_shape=[jax.ShapeDtypeStruct((rows, half), jnp.float32)] * count,
        compiler_params=pltpu.CompilerParams(vmem_limit_bytes=VMEM_LIMIT),
        name="forward",
        cost_estimate=LIGHT,
    )(*foot_own, *foot_other, flux_parts)
    return list(outs)


def adjoint_kernel(count, sides, first, start, place_ref, counts_ref, *refs):
    weighted, refs = refs[:count], refs[count:]
    foot, refs = refs[:sides * count], refs[sides * count:]
    before, refs = (None, refs) if first else (refs[:sides], refs[sides:])
    outs, (high_ref, low_ref, foot_high, foot_low) = refs[:sides], refs[sides:]
    rows, tile = foot[0].shape[-2:]

    taken, spots, filled = [], [], jnp.int32(0)
    for i in range(count):
        block = place_ref[1] + i
        number = counts_ref[jnp.minimum(block, place_ref[2] - 1)]
        taken.append(jnp.logical_and(block < place_ref[2], number > start))
        spots.append(pl.multiple_of(filled * rows, rows))
        filled = filled + taken[-1].astype(jnp.int32)

    for i in range(count):
        @pl.when(jnp.logical_and(taken[i], pl.program_id(0) == 0))
        def _(i=i):
            high, low = halves(weighted[i][...])
            high_ref[pl.ds(spots[i], rows), :] = high
            low_ref[pl.ds(spots[i], rows), :] = low

    dims = ((0,), (0,))
    for side in range(sides):
        for i in range(count):
            @pl.when(taken[i])
            def _(i=i):
                high, low = halves(foot[side * count + i][...].reshape(rows, tile))
                foot_high[side, pl.ds(spots[i], rows), :] = high
                foot_low[side, pl.ds(spots[i], rows), :] = low

    for number in range(count + 1):
        @pl.when(filled == number)
        def _(number=number):
            at = pl.ds(0, number * rows)
            for side in range(sides):
                if number == 0:
                    total = jnp.zeros(outs[side].shape, jnp.float32)
                else:
                    total = times(foot_high[side, at, :], high_ref[at, :], dims)
                    total = total + times(foot_low[side, at, :], high_ref[at, :], dims)
                    total = total + times(foot_high[side, at, :], low_ref[at, :], dims)
                if not first:
                    total = total + before[side][...]
                outs[side][...] = total


def adjoint(weighted, sides, start, place, counts, cells):
    count = len(weighted)
    rows, half = weighted[0].shape
    tile = min(TILE, cells)
    first = sides[0][2] is None
    out_specs = []
    for side in sides:
        if side[4]:
            out_specs.append(pl.BlockSpec((tile, half), lambda j, *c: (j, c[0][0])))
        else:
            out_specs.append(pl.BlockSpec((tile, half), lambda j, *c: (j, 0)))
    foot = [array for side in sides for array in side[0]]
    earlier = [] if first else [side[2] for side in sides]
    at = 2 + count + len(foot)
    return pl.pallas_call(
        functools.partial(adjoint_kernel, count, len(sides), first, start),
        grid_spec=pltpu.PrefetchScalarGridSpec(
            num_scalar_prefetch=2,
            grid=(cells // tile,),
            in_specs=[
                *[pl.BlockSpec((rows, half), lambda j, *c: (0, 0))] * count,
                *[spec(tile) for side in sides for spec in side[1]],
                *([] if first else out_specs),
            ],
            out_specs=out_specs,
            scratch_shapes=[
                *[pltpu.VMEM((count * rows, half), jnp.bfloat16)] * 2,
                *[pltpu.VMEM((len(sides), count * rows, tile), jnp.bfloat16)] * 2,
            ],
        ),
        out_shape=[jax.ShapeDtypeStruct((cells, side[3]), jnp.float32) for side in sides],
        input_output_aliases={} if first else {at + i: i for i in range(len(sides))},
        compiler_params=pltpu.CompilerParams(vmem_limit_bytes=VMEM_LIMIT),
        name="adjoint",
        cost_estimate=LIGHT,
    )(place, counts, *weighted, *foot, *earlier)


def through(buffer, sems, moves):
    loads = [pltpu.make_async_copy(a, buffer.at[i], sems.at[0, i]) for i, (a, _) in enumerate(moves)]
    stores = [pltpu.make_async_copy(buffer.at[i], b, sems.at[1, i]) for i, (_, b) in enumerate(moves)]
    for load in loads:
        load.start()
    for load, store in zip(loads, stores):
        load.wait()
        store.start()
    for store in stores:
        store.wait()


def passage(count, rows, columns):
    return [pltpu.VMEM((count, rows, columns), jnp.float32), pltpu.SemaphoreType.DMA((2, count))]


def cut_kernel(lags, r, footprint, *refs):
    outs, buffer, sems = refs[:-2], refs[-2], refs[-1]
    rows = outs[0].shape[0]
    through(buffer, sems, [
        (footprint.at[0, lag, pl.ds(r * rows, rows), :], out) for lag, out in zip(lags, outs)
    ])


def cut(footprint, lags, rows, r):
    return list(pl.pallas_call(
        functools.partial(cut_kernel, lags, r),
        in_specs=[IN_PLACE],
        out_specs=[IN_PLACE] * len(lags),
        scratch_shapes=passage(len(lags), rows, footprint.shape[3]),
        out_shape=[jax.ShapeDtypeStruct((rows, footprint.shape[3]), jnp.float32)] * len(lags),
        name="cut",
        cost_estimate=LIGHT,
    )(footprint))


def stack_kernel(*refs):
    pieces, out, buffer, sems = refs[:-3], refs[-3], refs[-2], refs[-1]
    rows = pieces[0].shape[0]
    through(buffer, sems, [(piece, out.at[pl.ds(i * rows, rows), :]) for i, piece in enumerate(pieces)])


def stack(pieces):
    rows, cells = pieces[0].shape
    return pl.pallas_call(
        stack_kernel,
        in_specs=[IN_PLACE] * len(pieces),
        out_specs=IN_PLACE,
        scratch_shapes=passage(len(pieces), rows, cells),
        out_shape=jax.ShapeDtypeStruct((rows * len(pieces), cells), jnp.float32),
        name="stack",
        cost_estimate=LIGHT,
    )(*pieces)


def side_kernel(parts, place_ref, flux, out, buffer, sems):
    cells, half = out.shape
    rows = cells // parts
    left = pl.multiple_of((1 - place_ref[0]) * half, 128)
    bands = [pl.ds(i * rows, rows) for i in range(parts)]
    through(buffer, sems, [(flux.at[0, at, pl.ds(left, half)], out.at[at, :]) for at in bands])


def side_of(flux, place):
    _, cells, width = flux.shape
    return pl.pallas_call(
        functools.partial(side_kernel, PARTS),
        in_specs=[pl.BlockSpec(memory_space=pltpu.SMEM), IN_PLACE],
        out_specs=IN_PLACE,
        scratch_shapes=passage(PARTS, cells // PARTS, width // 2),
        out_shape=jax.ShapeDtypeStruct((cells, width // 2), jnp.float32),
        name="side",
        cost_estimate=LIGHT,
    )(place, flux)


def combine_kernel(place_ref, scale, same, *refs):
    total = same[...]
    for lag, ref in enumerate(refs[:-1], 1):
        total = total + jnp.where(place_ref[1] >= lag, ref[...], 0.0)
    refs[-1][...] = scale[...] * total


def combine(scale, same, arrived, r, place):
    rows, half = same.shape
    tile = min(WIDE, half)
    block = pl.BlockSpec((rows, tile), lambda j, c: (0, j))
    return pl.pallas_call(
        combine_kernel,
        grid_spec=pltpu.PrefetchScalarGridSpec(
            num_scalar_prefetch=1,
            grid=(half // tile,),
            in_specs=[
                pl.BlockSpec((rows, 1), lambda j, c: (r, 0)),
                block,
                *[block] * len(arrived),
            ],
            out_specs=block,
        ),
        out_shape=jax.ShapeDtypeStruct((rows, half), jnp.float32),
        name="combine",
        cost_estimate=LIGHT,
    )(place, scale, same, *arrived)


def choose_kernel(r, place_ref, source, *refs):
    count = len(refs) // 2 - 1
    ups, outs, buffer, sems = refs[:count], refs[count:2 * count], refs[-2], refs[-1]
    rows = outs[0].shape[0]
    loads, stores = [], []
    for i, (up, out) in enumerate(zip(ups, outs)):
        down = source if r is None else source.at[0, i + 1, pl.ds(r * rows, rows), :]
        below = place_ref[1] > i
        loads.append([
            (below, pltpu.make_async_copy(down, buffer.at[i], sems.at[0, i])),
            (jnp.logical_not(below), pltpu.make_async_copy(up, buffer.at[i], sems.at[0, i])),
        ])
        stores.append(pltpu.make_async_copy(buffer.at[i], out, sems.at[1, i]))
    for pair in loads:
        for taken, load in pair:
            pl.when(taken)(load.start)
    for pair, store in zip(loads, stores):
        for taken, load in pair:
            pl.when(taken)(load.wait)
        store.start()
    for store in stores:
        store.wait()


def choose(place, source, r, up):
    rows, width = up[0].shape
    return list(pl.pallas_call(
        functools.partial(choose_kernel, r),
        in_specs=[pl.BlockSpec(memory_space=pltpu.SMEM)] + [IN_PLACE] * (1 + len(up)),
        out_specs=[IN_PLACE] * len(up),
        scratch_shapes=passage(len(up), rows, width),
        out_shape=[jax.ShapeDtypeStruct((rows, width), jnp.float32)] * len(up),
        name="choose",
        cost_estimate=LIGHT,
    )(place, source, *up))


def paste_kernel(parts, place_ref, arrived, before, out, buffer, sems):
    cells, half = arrived.shape
    rows = cells // parts
    left = pl.multiple_of((1 - place_ref[0]) * half, 128)
    bands = [pl.ds(i * rows, rows) for i in range(parts)]
    through(buffer, sems, [(arrived.at[at, :], out.at[at, pl.ds(left, half)]) for at in bands])


def paste(arrived, whole, place):
    cells, half = arrived.shape
    return pl.pallas_call(
        functools.partial(paste_kernel, PARTS),
        in_specs=[pl.BlockSpec(memory_space=pltpu.SMEM), IN_PLACE, IN_PLACE],
        out_specs=IN_PLACE,
        scratch_shapes=passage(PARTS, cells // PARTS, half),
        out_shape=jax.ShapeDtypeStruct(whole.shape, jnp.float32),
        input_output_aliases={2: 0},
        name="paste",
        cost_estimate=LIGHT,
    )(place, arrived, whole)


def on_device(footprint, flux, obs_weight, obs_count):
    _, lags, slots, cells = footprint.shape
    half = flux.shape[2] // 2
    rows = slots // CHUNKS
    chunks = range(CHUNKS)
    devices = lax.axis_size("tm")
    place = jnp.stack(
        [lax.axis_index("core"), lax.axis_index("tm"), jnp.int32(devices)]
    ).astype(jnp.int32)
    valid = (jnp.arange(slots, dtype=jnp.int32) < obs_count[0]).astype(jnp.float32)
    row_scale = (valid * obs_weight[0])[:, None]
    later = range(1, lags)
    counts = lax.all_gather(obs_count, "tm", tiled=True)
    paired = devices == lags and cells == half

    own, terms, weighted = [], [], []
    specs = [pl.BlockSpec((rows, cells), lambda j: (0, 0))] * len(later)
    other_specs = [pl.BlockSpec((rows, cells), lambda j, i=i: (i, 0)) for i in range(len(later))]

    def row_block(r, lag):
        return lambda tile: pl.BlockSpec((1, 1, rows, tile), lambda j, *c: (0, lag, r, j))

    def column(r):
        return lambda tile: pl.BlockSpec((rows, tile), lambda j, *c: (r, j))

    def payload(k):
        h, p, w = k, k - 2, k - 4
        up = terms[p] if 0 <= p < CHUNKS else []
        down = []
        if h < CHUNKS:
            if up and paired:
                return "one", choose(place, footprint, h, up[::-1])
            down = cut(footprint, later, rows, h)
        elif w >= 0:
            value = weighted[w]
            if w > 1:
                value, done[0] = together(value, done[0])
            if up and paired:
                return "one", choose(place, value, None, up[::-1])
            down = [value] * len(later)
        return ("down" if not up else "both" if down else "up"), [*down, *up]

    def exchange(kind, sent):
        lags_of = {"down": [-1], "up": [1], "both": [-1, 1]}.get(kind)
        if kind == "one":
            return [cycled(value, lag) for value, lag in zip(sent, later)]
        ways = [way * lag for way in lags_of for lag in later]
        return [shifted(value, by) for value, by in zip(sent, ways)]

    def sorted_out(kind, arrived):
        count = len(later)
        if kind == "one":
            return arrived, arrived[::-1]
        low = arrived[:count] if kind != "up" else None
        return low, arrived[-count:] if kind != "down" else None

    def my_side(r, before):
        return [footprint, *own[r]], [row_block(r, 0)] + [column(0)] * len(later), before, 2 * half, True

    def their_side(r, before):
        foot = [foot_other] + [other[r]] * len(later)
        return foot, [column(r)] + [column(i) for i in range(len(later))], before, half, False

    other, done = [], [None, None]
    kind, sent = payload(0)
    flux, sent[0] = together(flux, sent[0])
    flux_other = swapped(side_of(flux, place))
    foot_other = swapped(cut(footprint, [0], slots, 0)[0])
    for k in range(CHUNKS + 4):
        h, p, w = k, k - 2, k - 4
        arrived, sort = exchange(kind, sent), kind
        if k == 0:
            arrived[0], counts = together(arrived[0], counts)
            arrived[1], flux_other = together(arrived[1], flux_other)
            flux_parts = split(flux, flux_other, place)
            same = forward(
                [footprint] * CHUNKS,
                [pl.BlockSpec((1, 1, rows, cells), lambda j, r=r: (0, 0, r, 0)) for r in chunks],
                [foot_other] * CHUNKS,
                [pl.BlockSpec((rows, cells), lambda j, r=r: (r, 0)) for r in chunks],
                rows, flux_parts,
            )
        if k == 2:
            arrived[0], same[0] = together(arrived[0], same[0])
        if k + 1 < CHUNKS + 4:
            kind, sent = payload(k + 1)
            for i in range(min(len(sent), len(arrived))):
                arrived[i], sent[i] = together(arrived[i], sent[i])
        low, high = sorted_out(sort, arrived)
        if h < CHUNKS:
            own.append(low)
            other.append(swapped(stack(low)))
            terms.append(forward(low, specs, [other[h]] * len(later), other_specs, rows, flux_parts))
        if 0 <= p < CHUNKS:
            total = combine(row_scale, same[p], high, p, place)
            if p > 0:
                total, weighted[p - 1] = together(total, weighted[p - 1])
            weighted.append(lax.psum(total, "z"))
        if w >= 0:
            here = [weighted[w], *low]
            if w + 1 < CHUNKS:
                done[:] = adjoint(here, [my_side(w, done[0]), their_side(w, done[1])], w * rows, place, counts, cells)
    (theirs,) = adjoint(here, [their_side(w, done[1])], w * rows, place, counts, cells)
    (mine,) = adjoint(here, [my_side(w, done[0])], w * rows, place, counts, cells)
    return paste(swapped(theirs), mine, place)[None]


def solution(mesh):
    devices = mesh.devices
    split = Mesh(devices.reshape(devices.shape[0], devices.shape[1] // 2, 2), ("tm", "z", "core"))
    cells = ("z", "core")
    placed = (P("tm", None, None, cells), P("tm", cells, None), P("tm", None), P("tm"))
    return jax.shard_map(
        on_device, mesh=split, in_specs=placed, out_specs=P("tm", cells, None), check_vma=False
    )
```

```python
import functools

import jax
import jax.numpy as jnp
from jax import lax
from jax.experimental import pallas as pl
from jax.experimental.pallas import tpu as pltpu
from jax.sharding import Mesh, PartitionSpec as P

CHUNKS = 4
PARTS = 8
TILE = 256
WIDE = 512
LIGHT = pl.CostEstimate(flops=1, bytes_accessed=1, transcendentals=0)
IN_PLACE = pl.BlockSpec(memory_space=pl.ANY)
VMEM_LIMIT = 60 * 1024 * 1024


def shifted(value, by):
    devices = lax.axis_size("tm")
    pairs = [(i, i + by) for i in range(devices) if 0 <= i + by < devices]
    return lax.ppermute(value, "tm", pairs)


def cycled(value, by):
    devices = lax.axis_size("tm")
    return lax.ppermute(value, "tm", [(i, (i - by) % devices) for i in range(devices)])


def swapped(value):
    return lax.ppermute(value, "core", [(0, 1), (1, 0)])


def together(first, second):
    return lax.optimization_barrier((first, second))


def halves(value):
    high = value.astype(jnp.bfloat16)
    low = (value - high.astype(jnp.float32)).astype(jnp.bfloat16)
    return high, low


def times(left, right, dims):
    return lax.dot_general(left, right, (dims, ((), ())), preferred_element_type=jnp.float32)


def split_kernel(core_ref, own, other, out):
    cells = other.shape[0]
    for at, value in ((0, own[0]), (cells, other[...])):
        high, low = halves(value)
        for block, part in enumerate((high, high, low)):
            out[pl.ds(block * 2 * cells + at, cells), :] = part


def split(flux, flux_other, core):
    cells, half = flux_other.shape
    tile = min(TILE, half)
    steps = half // tile
    return pl.pallas_call(
        split_kernel,
        grid_spec=pltpu.PrefetchScalarGridSpec(
            num_scalar_prefetch=1,
            grid=(steps,),
            in_specs=[
                pl.BlockSpec((1, cells, tile), lambda j, c: (0, 0, c[0] * steps + j)),
                pl.BlockSpec((cells, tile), lambda j, c: (0, j)),
            ],
            out_specs=pl.BlockSpec((6 * cells, tile), lambda j, c: (0, j)),
        ),
        out_shape=jax.ShapeDtypeStruct((6 * cells, half), jnp.bfloat16),
        compiler_params=pltpu.CompilerParams(vmem_limit_bytes=VMEM_LIMIT),
        name="split",
        cost_estimate=LIGHT,
    )(core, flux, flux_other)


def forward_kernel(count, *refs):
    foot_own, foot_other = refs[:count], refs[count:2 * count]
    flux_parts, outs, parts_ref = refs[2 * count], refs[2 * count + 1:-1], refs[-1]
    rows, cells = foot_own[0].shape[-2:]

    @pl.when(pl.program_id(0) == 0)
    def _():
        for i in range(count):
            for side, source in ((0, foot_own[i]), (1, foot_other[i])):
                high, low = halves(source[...].reshape(rows, cells))
                for block, part in enumerate((high, low, high)):
                    columns = pl.ds((2 * block + side) * cells, cells)
                    parts_ref[pl.ds(i * rows, rows), columns] = part

    total = times(parts_ref[...], flux_parts[...], ((1,), (0,)))
    for i in range(count):
        outs[i][...] = total[i * rows:(i + 1) * rows]


def forward(foot_own, own_specs, foot_other, other_specs, rows, flux_parts):
    count = len(foot_own)
    depth, half = flux_parts.shape
    tile = min(TILE, half)
    outs = pl.pallas_call(
        functools.partial(forward_kernel, count),
        grid=(half // tile,),
        in_specs=[
            *own_specs,
            *other_specs,
            pl.BlockSpec((depth, tile), lambda j: (0, j)),
        ],
        out_specs=[pl.BlockSpec((rows, tile), lambda j: (0, j))] * count,
        scratch_shapes=[pltpu.VMEM((count * rows, depth), jnp.bfloat16)],
        out_shape=[jax.ShapeDtypeStruct((rows, half), jnp.float32)] * count,
        compiler_params=pltpu.CompilerParams(vmem_limit_bytes=VMEM_LIMIT),
        name="forward",
        cost_estimate=LIGHT,
    )(*foot_own, *foot_other, flux_parts)
    return list(outs)


def adjoint_kernel(count, sides, first, place_ref, *refs):
    weighted, refs = refs[:count], refs[count:]
    foot, refs = refs[:sides * count], refs[sides * count:]
    before, refs = (None, refs) if first else (refs[:sides], refs[sides:])
    outs, (high_ref, low_ref) = refs[:sides], refs[sides:]
    rows, tile = foot[0].shape[-2:]

    @pl.when(pl.program_id(0) == 0)
    def _():
        for i in range(count):
            value = jnp.where(place_ref[1] + i < place_ref[2], weighted[i][...], 0.0)
            high, low = halves(value)
            high_ref[pl.ds(i * rows, rows), :] = high
            low_ref[pl.ds(i * rows, rows), :] = low

    dims = ((0,), (0,))
    for side in range(sides):
        mine = foot[side * count:(side + 1) * count]
        slab = jnp.concatenate([ref[...].reshape(rows, tile) for ref in mine], axis=0)
        high, low = halves(slab)
        total = times(high, high_ref[...], dims)
        total = total + times(low, high_ref[...], dims)
        total = total + times(high, low_ref[...], dims)
        if not first:
            total = total + before[side][...]
        outs[side][...] = total


def adjoint(weighted, sides, place, cells):
    count = len(weighted)
    rows, half = weighted[0].shape
    tile = min(TILE, cells)
    first = sides[0][2] is None
    out_specs = []
    for side in sides:
        if side[4]:
            out_specs.append(pl.BlockSpec((tile, half), lambda j, c: (j, c[0])))
        else:
            out_specs.append(pl.BlockSpec((tile, half), lambda j, c: (j, 0)))
    foot = [array for side in sides for array in side[0]]
    earlier = [] if first else [side[2] for side in sides]
    at = 1 + count + len(foot)
    return pl.pallas_call(
        functools.partial(adjoint_kernel, count, len(sides), first),
        grid_spec=pltpu.PrefetchScalarGridSpec(
            num_scalar_prefetch=1,
            grid=(cells // tile,),
            in_specs=[
                *[pl.BlockSpec((rows, half), lambda j, c: (0, 0))] * count,
                *[spec(tile) for side in sides for spec in side[1]],
                *([] if first else out_specs),
            ],
            out_specs=out_specs,
            scratch_shapes=[pltpu.VMEM((count * rows, half), jnp.bfloat16)] * 2,
        ),
        out_shape=[jax.ShapeDtypeStruct((cells, side[3]), jnp.float32) for side in sides],
        input_output_aliases={} if first else {at + i: i for i in range(len(sides))},
        compiler_params=pltpu.CompilerParams(vmem_limit_bytes=VMEM_LIMIT),
        name="adjoint",
        cost_estimate=LIGHT,
    )(place, *weighted, *foot, *earlier)


def through(buffer, sems, moves):
    loads = [pltpu.make_async_copy(a, buffer.at[i], sems.at[0, i]) for i, (a, _) in enumerate(moves)]
    stores = [pltpu.make_async_copy(buffer.at[i], b, sems.at[1, i]) for i, (_, b) in enumerate(moves)]
    for load in loads:
        load.start()
    for load, store in zip(loads, stores):
        load.wait()
        store.start()
    for store in stores:
        store.wait()


def passage(count, rows, columns):
    return [pltpu.VMEM((count, rows, columns), jnp.float32), pltpu.SemaphoreType.DMA((2, count))]


def cut_kernel(lags, r, footprint, *refs):
    outs, buffer, sems = refs[:-2], refs[-2], refs[-1]
    rows = outs[0].shape[0]
    through(buffer, sems, [
        (footprint.at[0, lag, pl.ds(r * rows, rows), :], out) for lag, out in zip(lags, outs)
    ])


def cut(footprint, lags, rows, r):
    return list(pl.pallas_call(
        functools.partial(cut_kernel, lags, r),
        in_specs=[IN_PLACE],
        out_specs=[IN_PLACE] * len(lags),
        scratch_shapes=passage(len(lags), rows, footprint.shape[3]),
        out_shape=[jax.ShapeDtypeStruct((rows, footprint.shape[3]), jnp.float32)] * len(lags),
        name="cut",
        cost_estimate=LIGHT,
    )(footprint))


def stack_kernel(*refs):
    pieces, out, buffer, sems = refs[:-3], refs[-3], refs[-2], refs[-1]
    rows = pieces[0].shape[0]
    through(buffer, sems, [(piece, out.at[pl.ds(i * rows, rows), :]) for i, piece in enumerate(pieces)])


def stack(pieces):
    rows, cells = pieces[0].shape
    return pl.pallas_call(
        stack_kernel,
        in_specs=[IN_PLACE] * len(pieces),
        out_specs=IN_PLACE,
        scratch_shapes=passage(len(pieces), rows, cells),
        out_shape=jax.ShapeDtypeStruct((rows * len(pieces), cells), jnp.float32),
        name="stack",
        cost_estimate=LIGHT,
    )(*pieces)


def side_kernel(parts, place_ref, flux, out, buffer, sems):
    cells, half = out.shape
    rows = cells // parts
    left = pl.multiple_of((1 - place_ref[0]) * half, 128)
    bands = [pl.ds(i * rows, rows) for i in range(parts)]
    through(buffer, sems, [(flux.at[0, at, pl.ds(left, half)], out.at[at, :]) for at in bands])


def side_of(flux, place):
    _, cells, width = flux.shape
    return pl.pallas_call(
        functools.partial(side_kernel, PARTS),
        in_specs=[pl.BlockSpec(memory_space=pltpu.SMEM), IN_PLACE],
        out_specs=IN_PLACE,
        scratch_shapes=passage(PARTS, cells // PARTS, width // 2),
        out_shape=jax.ShapeDtypeStruct((cells, width // 2), jnp.float32),
        name="side",
        cost_estimate=LIGHT,
    )(place, flux)


def meet_kernel(lows, highs, chosen, place_ref, scale, same, *refs):
    count = len(highs)
    refs = list(refs)
    arrived = [refs.pop(0) for _ in range(max(lows + highs) + 1)]
    source = refs.pop(0) if chosen else None
    ups = [refs.pop(0) for _ in range(count)] if chosen else []
    total = refs.pop(0)
    stacked = refs.pop(0) if lows else None
    outs = [refs.pop(0) for _ in range(count)] if chosen else []
    held, base, sum_ref, picked, sems = refs
    rows = same.shape[0]

    loads = [pltpu.make_async_copy(a, held.at[i], sems.at[0, i]) for i, a in enumerate(arrived)]
    base_load = pltpu.make_async_copy(same, base, sems.at[1, 0])
    for load in [*loads, base_load]:
        load.start()
    picks = []
    for i, up in enumerate(ups):
        below = place_ref[1] > i
        picks.append((below, pltpu.make_async_copy(source, picked.at[i], sems.at[2, i])))
        picks.append((jnp.logical_not(below), pltpu.make_async_copy(up, picked.at[i], sems.at[2, i])))
    for taken, pick in picks:
        pl.when(taken)(pick.start)
    for load in [*loads, base_load]:
        load.wait()

    value = base[...]
    for lag, i in enumerate(highs, 1):
        value = value + jnp.where(place_ref[1] >= lag, held[i], 0.0)
    sum_ref[...] = scale[...] * value
    stores = [pltpu.make_async_copy(sum_ref, total, sems.at[1, 1])]
    stores[0].start()
    for n, i in enumerate(lows):
        stores.append(pltpu.make_async_copy(
            held.at[i], stacked.at[pl.ds(n * rows, rows), :], sems.at[3, n]
        ))
        stores[-1].start()
    for taken, pick in picks:
        pl.when(taken)(pick.wait)
    for i, out in enumerate(outs):
        stores.append(pltpu.make_async_copy(picked.at[i], out, sems.at[4, i]))
        stores[-1].start()
    for store in stores:
        store.wait()


def meet(place, scale, same, arrived, lows, highs, source, ups):
    rows, half = same.shape
    count = len(highs)
    chosen = source is not None
    shape = jax.ShapeDtypeStruct((rows, half), jnp.float32)
    outs = [shape]
    if lows:
        outs.append(jax.ShapeDtypeStruct((count * rows, arrived[lows[0]].shape[1]), jnp.float32))
    if chosen:
        outs += [shape] * count
    extra = [source, *ups] if chosen else []
    outs = list(pl.pallas_call(
        functools.partial(meet_kernel, lows, highs, chosen),
        in_specs=[
            pl.BlockSpec(memory_space=pltpu.SMEM),
            pl.BlockSpec(memory_space=pltpu.VMEM),
            *[IN_PLACE] * (1 + len(arrived) + len(extra)),
        ],
        out_specs=[IN_PLACE] * len(outs),
        scratch_shapes=[
            pltpu.VMEM((len(arrived), rows, half), jnp.float32),
            pltpu.VMEM((rows, half), jnp.float32),
            pltpu.VMEM((rows, half), jnp.float32),
            pltpu.VMEM((count, rows, half), jnp.float32),
            pltpu.SemaphoreType.DMA((5, max(len(arrived), 2))),
        ],
        out_shape=outs,
        compiler_params=pltpu.CompilerParams(vmem_limit_bytes=VMEM_LIMIT),
        name="meet",
        cost_estimate=LIGHT,
    )(place, scale, same, *arrived, *extra))
    total = outs.pop(0)
    stacked = outs.pop(0) if lows else None
    return total, stacked, outs


def choose_kernel(r, place_ref, source, *refs):
    count = len(refs) // 2 - 1
    ups, outs, buffer, sems = refs[:count], refs[count:2 * count], refs[-2], refs[-1]
    rows = outs[0].shape[0]
    loads, stores = [], []
    for i, (up, out) in enumerate(zip(ups, outs)):
        down = source if r is None else source.at[0, i + 1, pl.ds(r * rows, rows), :]
        below = place_ref[1] > i
        loads.append([
            (below, pltpu.make_async_copy(down, buffer.at[i], sems.at[0, i])),
            (jnp.logical_not(below), pltpu.make_async_copy(up, buffer.at[i], sems.at[0, i])),
        ])
        stores.append(pltpu.make_async_copy(buffer.at[i], out, sems.at[1, i]))
    for pair in loads:
        for taken, load in pair:
            pl.when(taken)(load.start)
    for pair, store in zip(loads, stores):
        for taken, load in pair:
            pl.when(taken)(load.wait)
        store.start()
    for store in stores:
        store.wait()


def choose(place, source, r, up):
    rows, width = up[0].shape
    return list(pl.pallas_call(
        functools.partial(choose_kernel, r),
        in_specs=[pl.BlockSpec(memory_space=pltpu.SMEM)] + [IN_PLACE] * (1 + len(up)),
        out_specs=[IN_PLACE] * len(up),
        scratch_shapes=passage(len(up), rows, width),
        out_shape=[jax.ShapeDtypeStruct((rows, width), jnp.float32)] * len(up),
        name="choose",
        cost_estimate=LIGHT,
    )(place, source, *up))


def paste_kernel(parts, place_ref, arrived, before, out, buffer, sems):
    cells, half = arrived.shape
    rows = cells // parts
    left = pl.multiple_of((1 - place_ref[0]) * half, 128)
    bands = [pl.ds(i * rows, rows) for i in range(parts)]
    through(buffer, sems, [(arrived.at[at, :], out.at[at, pl.ds(left, half)]) for at in bands])


def paste(arrived, whole, place):
    cells, half = arrived.shape
    return pl.pallas_call(
        functools.partial(paste_kernel, PARTS),
        in_specs=[pl.BlockSpec(memory_space=pltpu.SMEM), IN_PLACE, IN_PLACE],
        out_specs=IN_PLACE,
        scratch_shapes=passage(PARTS, cells // PARTS, half),
        out_shape=jax.ShapeDtypeStruct(whole.shape, jnp.float32),
        input_output_aliases={2: 0},
        name="paste",
        cost_estimate=LIGHT,
    )(place, arrived, whole)


def on_device(footprint, flux, obs_weight, obs_count):
    _, lags, slots, cells = footprint.shape
    half = flux.shape[2] // 2
    rows = slots // CHUNKS
    chunks = range(CHUNKS)
    devices = lax.axis_size("tm")
    place = jnp.stack(
        [lax.axis_index("core"), lax.axis_index("tm"), jnp.int32(devices)]
    ).astype(jnp.int32)
    valid = (jnp.arange(slots, dtype=jnp.int32) < obs_count[0]).astype(jnp.float32)
    row_scale = (valid * obs_weight[0])[:, None]
    later = range(1, lags)
    paired = devices == lags and cells == half

    own, terms, weighted = [], [], []
    specs = [pl.BlockSpec((rows, cells), lambda j: (0, 0))] * len(later)
    other_specs = [pl.BlockSpec((rows, cells), lambda j, i=i: (i, 0)) for i in range(len(later))]

    def row_block(r, lag):
        return lambda tile: pl.BlockSpec((1, 1, rows, tile), lambda j, c: (0, lag, r, j))

    def column(r):
        return lambda tile: pl.BlockSpec((rows, tile), lambda j, c: (r, j))

    def payload(k):
        h, p, w = k, k - 2, k - 4
        up = terms[p] if 0 <= p < CHUNKS else []
        down = []
        if h < CHUNKS:
            if up and paired:
                return "one", choose(place, footprint, h, up[::-1])
            down = cut(footprint, later, rows, h)
        elif w >= 0:
            value = weighted[w]
            if w > 1:
                value, done[0] = together(value, done[0])
            if up and paired:
                return "one", choose(place, value, None, up[::-1])
            down = [value] * len(later)
        return ("down" if not up else "both" if down else "up"), [*down, *up]

    def exchange(kind, sent):
        lags_of = {"down": [-1], "up": [1], "both": [-1, 1]}.get(kind)
        if kind == "one":
            return [cycled(value, lag) for value, lag in zip(sent, later)]
        ways = [way * lag for way in lags_of for lag in later]
        return [shifted(value, by) for value, by in zip(sent, ways)]

    def sorted_out(kind, arrived):
        count = len(later)
        if kind == "one":
            return arrived, arrived[::-1]
        low = arrived[:count] if kind != "up" else None
        return low, arrived[-count:] if kind != "down" else None

    def my_side(r, before):
        return [footprint, *own[r]], [row_block(r, 0)] + [column(0)] * len(later), before, 2 * half, True

    def their_side(r, before):
        foot = [foot_other] + [other[r]] * len(later)
        return foot, [column(r)] + [column(i) for i in range(len(later))], before, half, False

    other, done = [], [None, None]
    kind, sent = payload(0)
    flux, sent[0] = together(flux, sent[0])
    flux_other = swapped(side_of(flux, place))
    foot_other = swapped(cut(footprint, [0], slots, 0)[0])
    for k in range(CHUNKS + 4):
        h, p, w = k, k - 2, k - 4
        arrived, sort = exchange(kind, sent), kind
        if k == 0:
            arrived[1], flux_other = together(arrived[1], flux_other)
            flux_parts = split(flux, flux_other, place)
            same = forward(
                [footprint] * CHUNKS,
                [pl.BlockSpec((1, 1, rows, cells), lambda j, r=r: (0, 0, r, 0)) for r in chunks],
                [foot_other] * CHUNKS,
                [pl.BlockSpec((rows, cells), lambda j, r=r: (r, 0)) for r in chunks],
                rows, flux_parts,
            )
        if k == 2:
            arrived[0], same[0] = together(arrived[0], same[0])
        here_up = 0 <= p < CHUNKS
        late = paired and CHUNKS <= k + 1 < CHUNKS + 2 and here_up
        if k + 1 < CHUNKS + 4 and not late:
            kind, sent = payload(k + 1)
            for i in range(min(len(sent), len(arrived))):
                arrived[i], sent[i] = together(arrived[i], sent[i])
        low, high = sorted_out(sort, arrived)
        stacked = None
        if here_up:
            count = len(later)
            if not paired and low is not None and cells != half:
                total, _, _ = meet(place, row_scale[p * rows:(p + 1) * rows], same[p], high, [], list(range(count)), None, [])
            else:
                lows = list(range(count)) if h < CHUNKS else []
                highs = list(range(count))[::-1] if sort == "one" else list(range(len(arrived) - count, len(arrived)))
                source = weighted[k - 3] if late else None
                ups = terms[k - 1][::-1] if late else []
                total, stacked, made = meet(
                    place, row_scale[p * rows:(p + 1) * rows], same[p], arrived, lows, highs, source, ups
                )
                if late:
                    kind, sent = "one", made
            if p > 0:
                total, weighted[p - 1] = together(total, weighted[p - 1])
            weighted.append(lax.psum(total, "z"))
        if h < CHUNKS:
            own.append(low)
            other.append(swapped(stack(low) if stacked is None else stacked))
            terms.append(forward(low, specs, [other[h]] * len(later), other_specs, rows, flux_parts))
        if w >= 0:
            here = [weighted[w], *low]
            if w + 1 < CHUNKS:
                done[:] = adjoint(here, [my_side(w, done[0]), their_side(w, done[1])], place, cells)
    (theirs,) = adjoint(here, [their_side(w, done[1])], place, cells)
    (mine,) = adjoint(here, [my_side(w, done[0])], place, cells)
    return paste(swapped(theirs), mine, place)[None]


def solution(mesh):
    devices = mesh.devices
    split = Mesh(devices.reshape(devices.shape[0], devices.shape[1] // 2, 2), ("tm", "z", "core"))
    cells = ("z", "core")
    placed = (P("tm", None, None, cells), P("tm", cells, None), P("tm", None), P("tm"))
    return jax.shard_map(
        on_device, mesh=split, in_specs=placed, out_specs=P("tm", cells, None), check_vma=False
    )
```

```python
import functools

import jax
import jax.numpy as jnp
from jax import lax
from jax.experimental import pallas as pl
from jax.experimental.pallas import tpu as pltpu
from jax.sharding import Mesh, PartitionSpec as P

CHUNKS = 4
PARTS = 8
TILE = 256
WIDE = 512
LIGHT = pl.CostEstimate(flops=1, bytes_accessed=1, transcendentals=0)
IN_PLACE = pl.BlockSpec(memory_space=pl.ANY)
VMEM_LIMIT = 60 * 1024 * 1024


def shifted(value, by):
    devices = lax.axis_size("tm")
    pairs = [(i, i + by) for i in range(devices) if 0 <= i + by < devices]
    return lax.ppermute(value, "tm", pairs)


def cycled(value, by):
    devices = lax.axis_size("tm")
    return lax.ppermute(value, "tm", [(i, (i - by) % devices) for i in range(devices)])


def swapped(value):
    return lax.ppermute(value, "core", [(0, 1), (1, 0)])


def together(first, second):
    return lax.optimization_barrier((first, second))


def halves(value):
    high = value.astype(jnp.bfloat16)
    low = (value - high.astype(jnp.float32)).astype(jnp.bfloat16)
    return high, low


def times(left, right, dims):
    return lax.dot_general(left, right, (dims, ((), ())), preferred_element_type=jnp.float32)


def split_kernel(core_ref, own, other, out):
    cells = other.shape[0]
    for at, value in ((0, own[0]), (cells, other[...])):
        high, low = halves(value)
        for block, part in enumerate((high, high, low)):
            out[pl.ds(block * 2 * cells + at, cells), :] = part


def split(flux, flux_other, core):
    cells, half = flux_other.shape
    tile = min(TILE, half)
    steps = half // tile
    return pl.pallas_call(
        split_kernel,
        grid_spec=pltpu.PrefetchScalarGridSpec(
            num_scalar_prefetch=1,
            grid=(steps,),
            in_specs=[
                pl.BlockSpec((1, cells, tile), lambda j, c: (0, 0, c[0] * steps + j)),
                pl.BlockSpec((cells, tile), lambda j, c: (0, j)),
            ],
            out_specs=pl.BlockSpec((6 * cells, tile), lambda j, c: (0, j)),
        ),
        out_shape=jax.ShapeDtypeStruct((6 * cells, half), jnp.bfloat16),
        compiler_params=pltpu.CompilerParams(vmem_limit_bytes=VMEM_LIMIT),
        name="split",
        cost_estimate=LIGHT,
    )(core, flux, flux_other)


def forward_kernel(count, *refs):
    foot_own, foot_other = refs[:count], refs[count:2 * count]
    flux_parts, outs, parts_ref = refs[2 * count], refs[2 * count + 1:-1], refs[-1]
    rows, cells = foot_own[0].shape[-2:]

    @pl.when(pl.program_id(0) == 0)
    def _():
        for i in range(count):
            for side, source in ((0, foot_own[i]), (1, foot_other[i])):
                high, low = halves(source[...].reshape(rows, cells))
                for block, part in enumerate((high, low, high)):
                    columns = pl.ds((2 * block + side) * cells, cells)
                    parts_ref[pl.ds(i * rows, rows), columns] = part

    total = times(parts_ref[...], flux_parts[...], ((1,), (0,)))
    for i in range(count):
        outs[i][...] = total[i * rows:(i + 1) * rows]


def forward(foot_own, own_specs, foot_other, other_specs, rows, flux_parts):
    count = len(foot_own)
    depth, half = flux_parts.shape
    tile = min(TILE, half)
    outs = pl.pallas_call(
        functools.partial(forward_kernel, count),
        grid=(half // tile,),
        in_specs=[
            *own_specs,
            *other_specs,
            pl.BlockSpec((depth, tile), lambda j: (0, j)),
        ],
        out_specs=[pl.BlockSpec((rows, tile), lambda j: (0, j))] * count,
        scratch_shapes=[pltpu.VMEM((count * rows, depth), jnp.bfloat16)],
        out_shape=[jax.ShapeDtypeStruct((rows, half), jnp.float32)] * count,
        compiler_params=pltpu.CompilerParams(vmem_limit_bytes=VMEM_LIMIT),
        name="forward",
        cost_estimate=LIGHT,
    )(*foot_own, *foot_other, flux_parts)
    return list(outs)


def adjoint_kernel(count, sides, first, place_ref, *refs):
    weighted, refs = refs[:count], refs[count:]
    foot, refs = refs[:sides * count], refs[sides * count:]
    before, refs = (None, refs) if first else (refs[:sides], refs[sides:])
    outs, (high_ref, low_ref) = refs[:sides], refs[sides:]
    rows, tile = foot[0].shape[-2:]

    @pl.when(pl.program_id(0) == 0)
    def _():
        for i in range(count):
            value = jnp.where(place_ref[1] + i < place_ref[2], weighted[i][...], 0.0)
            high, low = halves(value)
            high_ref[pl.ds(i * rows, rows), :] = high
            low_ref[pl.ds(i * rows, rows), :] = low

    dims = ((0,), (0,))
    for side in range(sides):
        mine = foot[side * count:(side + 1) * count]
        slab = jnp.concatenate([ref[...].reshape(rows, tile) for ref in mine], axis=0)
        high, low = halves(slab)
        total = times(high, high_ref[...], dims)
        total = total + times(low, high_ref[...], dims)
        total = total + times(high, low_ref[...], dims)
        if not first:
            total = total + before[side][...]
        outs[side][...] = total


def adjoint(weighted, sides, place, cells):
    count = len(weighted)
    rows, half = weighted[0].shape
    tile = min(TILE, cells)
    first = sides[0][2] is None
    out_specs = []
    for side in sides:
        if side[4]:
            out_specs.append(pl.BlockSpec((tile, half), lambda j, c: (j, c[0])))
        else:
            out_specs.append(pl.BlockSpec((tile, half), lambda j, c: (j, 0)))
    foot = [array for side in sides for array in side[0]]
    earlier = [] if first else [side[2] for side in sides]
    at = 1 + count + len(foot)
    return pl.pallas_call(
        functools.partial(adjoint_kernel, count, len(sides), first),
        grid_spec=pltpu.PrefetchScalarGridSpec(
            num_scalar_prefetch=1,
            grid=(cells // tile,),
            in_specs=[
                *[pl.BlockSpec((rows, half), lambda j, c: (0, 0))] * count,
                *[spec(tile) for side in sides for spec in side[1]],
                *([] if first else out_specs),
            ],
            out_specs=out_specs,
            scratch_shapes=[pltpu.VMEM((count * rows, half), jnp.bfloat16)] * 2,
        ),
        out_shape=[jax.ShapeDtypeStruct((cells, side[3]), jnp.float32) for side in sides],
        input_output_aliases={} if first else {at + i: i for i in range(len(sides))},
        compiler_params=pltpu.CompilerParams(vmem_limit_bytes=VMEM_LIMIT),
        name="adjoint",
        cost_estimate=LIGHT,
    )(place, *weighted, *foot, *earlier)


def through(*passages):
    loads, stores = [], []
    for buffer, sems, moves in passages:
        for i, (source, target) in enumerate(moves):
            loads.append(pltpu.make_async_copy(source, buffer.at[i], sems.at[0, i]))
            stores.append(pltpu.make_async_copy(buffer.at[i], target, sems.at[1, i]))
    for load in loads:
        load.start()
    for load, store in zip(loads, stores):
        load.wait()
        store.start()
    for store in stores:
        store.wait()


def passage(count, rows, columns):
    return [pltpu.VMEM((count, rows, columns), jnp.float32), pltpu.SemaphoreType.DMA((2, count))]


def cut_kernel(lags, r, footprint, *refs):
    outs, buffer, sems = refs[:-2], refs[-2], refs[-1]
    rows = outs[0].shape[0]
    moves = [(footprint.at[0, lag, pl.ds(r * rows, rows), :], out) for lag, out in zip(lags, outs)]
    through((buffer, sems, moves))


def cut(footprint, lags, rows, r):
    return list(pl.pallas_call(
        functools.partial(cut_kernel, lags, r),
        in_specs=[IN_PLACE],
        out_specs=[IN_PLACE] * len(lags),
        scratch_shapes=passage(len(lags), rows, footprint.shape[3]),
        out_shape=[jax.ShapeDtypeStruct((rows, footprint.shape[3]), jnp.float32)] * len(lags),
        name="cut",
        cost_estimate=LIGHT,
    )(footprint))


def stack_kernel(*refs):
    pieces, out, buffer, sems = refs[:-3], refs[-3], refs[-2], refs[-1]
    rows = pieces[0].shape[0]
    moves = [(piece, out.at[pl.ds(i * rows, rows), :]) for i, piece in enumerate(pieces)]
    through((buffer, sems, moves))


def stack(pieces):
    rows, cells = pieces[0].shape
    return pl.pallas_call(
        stack_kernel,
        in_specs=[IN_PLACE] * len(pieces),
        out_specs=IN_PLACE,
        scratch_shapes=passage(len(pieces), rows, cells),
        out_shape=jax.ShapeDtypeStruct((rows * len(pieces), cells), jnp.float32),
        name="stack",
        cost_estimate=LIGHT,
    )(*pieces)


def opening_kernel(lags, place_ref, footprint, flux, *refs):
    pieces, (side, buffer, sems, side_buffer, side_sems) = refs[:len(lags)], refs[len(lags):]
    rows = pieces[0].shape[0]
    cells, half = side.shape
    band = cells // PARTS
    left = pl.multiple_of((1 - place_ref[0]) * half, 128)
    bands = [pl.ds(i * band, band) for i in range(PARTS)]
    through(
        (buffer, sems, [(footprint.at[0, lag, pl.ds(0, rows), :], out) for lag, out in zip(lags, pieces)]),
        (side_buffer, side_sems, [(flux.at[0, at, pl.ds(left, half)], side.at[at, :]) for at in bands]),
    )


def opening(footprint, flux, lags, rows, place):
    _, cells, width = flux.shape
    outs = pl.pallas_call(
        functools.partial(opening_kernel, lags),
        in_specs=[pl.BlockSpec(memory_space=pltpu.SMEM), IN_PLACE, IN_PLACE],
        out_specs=[IN_PLACE] * (len(lags) + 1),
        scratch_shapes=[
            *passage(len(lags), rows, footprint.shape[3]),
            *passage(PARTS, cells // PARTS, width // 2),
        ],
        out_shape=[
            *[jax.ShapeDtypeStruct((rows, footprint.shape[3]), jnp.float32)] * len(lags),
            jax.ShapeDtypeStruct((cells, width // 2), jnp.float32),
        ],
        name="opening",
        cost_estimate=LIGHT,
    )(place, footprint, flux)
    return list(outs[:-1]), outs[-1]


def meet_kernel(lows, highs, chosen, place_ref, scale, same, *refs):
    count = len(highs)
    refs = list(refs)
    arrived = [refs.pop(0) for _ in range(max(lows + highs) + 1)]
    source = refs.pop(0) if chosen else None
    ups = [refs.pop(0) for _ in range(count)] if chosen else []
    total = refs.pop(0)
    stacked = refs.pop(0) if lows else None
    outs = [refs.pop(0) for _ in range(count)] if chosen else []
    held, base, sum_ref, picked, sems = refs
    rows = same.shape[0]

    loads = [pltpu.make_async_copy(a, held.at[i], sems.at[0, i]) for i, a in enumerate(arrived)]
    base_load = pltpu.make_async_copy(same, base, sems.at[1, 0])
    for load in [*loads, base_load]:
        load.start()
    picks = []
    for i, up in enumerate(ups):
        below = place_ref[1] > i
        picks.append((below, pltpu.make_async_copy(source, picked.at[i], sems.at[2, i])))
        picks.append((jnp.logical_not(below), pltpu.make_async_copy(up, picked.at[i], sems.at[2, i])))
    for taken, pick in picks:
        pl.when(taken)(pick.start)
    for load in [*loads, base_load]:
        load.wait()

    value = base[...]
    for lag, i in enumerate(highs, 1):
        value = value + jnp.where(place_ref[1] >= lag, held[i], 0.0)
    sum_ref[...] = scale[...] * value
    stores = [pltpu.make_async_copy(sum_ref, total, sems.at[1, 1])]
    stores[0].start()
    for n, i in enumerate(lows):
        stores.append(pltpu.make_async_copy(
            held.at[i], stacked.at[pl.ds(n * rows, rows), :], sems.at[3, n]
        ))
        stores[-1].start()
    for taken, pick in picks:
        pl.when(taken)(pick.wait)
    for i, out in enumerate(outs):
        stores.append(pltpu.make_async_copy(picked.at[i], out, sems.at[4, i]))
        stores[-1].start()
    for store in stores:
        store.wait()


def meet(place, scale, same, arrived, lows, highs, source, ups):
    rows, half = same.shape
    count = len(highs)
    chosen = source is not None
    shape = jax.ShapeDtypeStruct((rows, half), jnp.float32)
    outs = [shape]
    if lows:
        outs.append(jax.ShapeDtypeStruct((count * rows, arrived[lows[0]].shape[1]), jnp.float32))
    if chosen:
        outs += [shape] * count
    extra = [source, *ups] if chosen else []
    outs = list(pl.pallas_call(
        functools.partial(meet_kernel, lows, highs, chosen),
        in_specs=[
            pl.BlockSpec(memory_space=pltpu.SMEM),
            pl.BlockSpec(memory_space=pltpu.VMEM),
            *[IN_PLACE] * (1 + len(arrived) + len(extra)),
        ],
        out_specs=[IN_PLACE] * len(outs),
        scratch_shapes=[
            pltpu.VMEM((len(arrived), rows, half), jnp.float32),
            pltpu.VMEM((rows, half), jnp.float32),
            pltpu.VMEM((rows, half), jnp.float32),
            pltpu.VMEM((count, rows, half), jnp.float32),
            pltpu.SemaphoreType.DMA((5, max(len(arrived), 2))),
        ],
        out_shape=outs,
        compiler_params=pltpu.CompilerParams(vmem_limit_bytes=VMEM_LIMIT),
        name="meet",
        cost_estimate=LIGHT,
    )(place, scale, same, *arrived, *extra))
    total = outs.pop(0)
    stacked = outs.pop(0) if lows else None
    return total, stacked, outs


def choose_kernel(r, place_ref, source, *refs):
    count = len(refs) // 2 - 1
    ups, outs, buffer, sems = refs[:count], refs[count:2 * count], refs[-2], refs[-1]
    rows = outs[0].shape[0]
    loads, stores = [], []
    for i, (up, out) in enumerate(zip(ups, outs)):
        down = source if r is None else source.at[0, i + 1, pl.ds(r * rows, rows), :]
        below = place_ref[1] > i
        loads.append([
            (below, pltpu.make_async_copy(down, buffer.at[i], sems.at[0, i])),
            (jnp.logical_not(below), pltpu.make_async_copy(up, buffer.at[i], sems.at[0, i])),
        ])
        stores.append(pltpu.make_async_copy(buffer.at[i], out, sems.at[1, i]))
    for pair in loads:
        for taken, load in pair:
            pl.when(taken)(load.start)
    for pair, store in zip(loads, stores):
        for taken, load in pair:
            pl.when(taken)(load.wait)
        store.start()
    for store in stores:
        store.wait()


def choose(place, source, r, up):
    rows, width = up[0].shape
    return list(pl.pallas_call(
        functools.partial(choose_kernel, r),
        in_specs=[pl.BlockSpec(memory_space=pltpu.SMEM)] + [IN_PLACE] * (1 + len(up)),
        out_specs=[IN_PLACE] * len(up),
        scratch_shapes=passage(len(up), rows, width),
        out_shape=[jax.ShapeDtypeStruct((rows, width), jnp.float32)] * len(up),
        name="choose",
        cost_estimate=LIGHT,
    )(place, source, *up))


def paste_kernel(parts, place_ref, arrived, before, out, buffer, sems):
    cells, half = arrived.shape
    rows = cells // parts
    left = pl.multiple_of((1 - place_ref[0]) * half, 128)
    bands = [pl.ds(i * rows, rows) for i in range(parts)]
    through((buffer, sems, [(arrived.at[at, :], out.at[at, pl.ds(left, half)]) for at in bands]))


def paste(arrived, whole, place):
    cells, half = arrived.shape
    return pl.pallas_call(
        functools.partial(paste_kernel, PARTS),
        in_specs=[pl.BlockSpec(memory_space=pltpu.SMEM), IN_PLACE, IN_PLACE],
        out_specs=IN_PLACE,
        scratch_shapes=passage(PARTS, cells // PARTS, half),
        out_shape=jax.ShapeDtypeStruct(whole.shape, jnp.float32),
        input_output_aliases={2: 0},
        name="paste",
        cost_estimate=LIGHT,
    )(place, arrived, whole)


def on_device(footprint, flux, obs_weight, obs_count):
    _, lags, slots, cells = footprint.shape
    half = flux.shape[2] // 2
    rows = slots // CHUNKS
    chunks = range(CHUNKS)
    devices = lax.axis_size("tm")
    place = jnp.stack(
        [lax.axis_index("core"), lax.axis_index("tm"), jnp.int32(devices)]
    ).astype(jnp.int32)
    valid = (jnp.arange(slots, dtype=jnp.int32) < obs_count[0]).astype(jnp.float32)
    row_scale = (valid * obs_weight[0])[:, None]
    later = range(1, lags)
    paired = devices == lags and cells == half

    own, terms, weighted = [], [], []
    specs = [pl.BlockSpec((rows, cells), lambda j: (0, 0))] * len(later)
    other_specs = [pl.BlockSpec((rows, cells), lambda j, i=i: (i, 0)) for i in range(len(later))]

    def row_block(r, lag):
        return lambda tile: pl.BlockSpec((1, 1, rows, tile), lambda j, c: (0, lag, r, j))

    def column(r):
        return lambda tile: pl.BlockSpec((rows, tile), lambda j, c: (r, j))

    def payload(k):
        h, p, w = k, k - 2, k - 4
        up = terms[p] if 0 <= p < CHUNKS else []
        down = []
        if h < CHUNKS:
            if up and paired:
                return "one", choose(place, footprint, h, up[::-1])
            down = cut(footprint, later, rows, h)
        elif w >= 0:
            value = weighted[w]
            if w > 1:
                value, done[0] = together(value, done[0])
            if up and paired:
                return "one", choose(place, value, None, up[::-1])
            down = [value] * len(later)
        return ("down" if not up else "both" if down else "up"), [*down, *up]

    def exchange(kind, sent):
        lags_of = {"down": [-1], "up": [1], "both": [-1, 1]}.get(kind)
        if kind == "one":
            return [cycled(value, lag) for value, lag in zip(sent, later)]
        ways = [way * lag for way in lags_of for lag in later]
        return [shifted(value, by) for value, by in zip(sent, ways)]

    def sorted_out(kind, arrived):
        count = len(later)
        if kind == "one":
            return arrived, arrived[::-1]
        low = arrived[:count] if kind != "up" else None
        return low, arrived[-count:] if kind != "down" else None

    def my_side(r, before):
        return [footprint, *own[r]], [row_block(r, 0)] + [column(0)] * len(later), before, 2 * half, True

    def their_side(r, before):
        foot = [foot_other] + [other[r]] * len(later)
        return foot, [column(r)] + [column(i) for i in range(len(later))], before, half, False

    other, done = [], [None, None]
    kind = "down"
    sent, side = opening(footprint, flux, later, rows, place)
    flux_other = swapped(side)
    foot_other = swapped(cut(footprint, [0], slots, 0)[0])
    for k in range(CHUNKS + 4):
        h, p, w = k, k - 2, k - 4
        arrived, sort = exchange(kind, sent), kind
        if k == 0:
            arrived[1], flux_other = together(arrived[1], flux_other)
            flux_parts = split(flux, flux_other, place)
            same = forward(
                [footprint] * CHUNKS,
                [pl.BlockSpec((1, 1, rows, cells), lambda j, r=r: (0, 0, r, 0)) for r in chunks],
                [foot_other] * CHUNKS,
                [pl.BlockSpec((rows, cells), lambda j, r=r: (r, 0)) for r in chunks],
                rows, flux_parts,
            )
        if k == 2:
            arrived[0], same[0] = together(arrived[0], same[0])
        here_up = 0 <= p < CHUNKS
        late = paired and CHUNKS <= k + 1 < CHUNKS + 2 and here_up
        if k + 1 < CHUNKS + 4 and not late:
            kind, sent = payload(k + 1)
            for i in range(min(len(sent), len(arrived))):
                arrived[i], sent[i] = together(arrived[i], sent[i])
        low, high = sorted_out(sort, arrived)
        stacked = None
        if here_up:
            count = len(later)
            if not paired and low is not None and cells != half:
                total, _, _ = meet(place, row_scale[p * rows:(p + 1) * rows], same[p], high, [], list(range(count)), None, [])
            else:
                lows = list(range(count)) if h < CHUNKS else []
                highs = list(range(count))[::-1] if sort == "one" else list(range(len(arrived) - count, len(arrived)))
                source = weighted[k - 3] if late else None
                ups = terms[k - 1][::-1] if late else []
                total, stacked, made = meet(
                    place, row_scale[p * rows:(p + 1) * rows], same[p], arrived, lows, highs, source, ups
                )
                if late:
                    kind, sent = "one", made
            if p > 0:
                total, weighted[p - 1] = together(total, weighted[p - 1])
            weighted.append(lax.psum(total, "z"))
        if h < CHUNKS:
            own.append(low)
            other.append(swapped(stack(low) if stacked is None else stacked))
            terms.append(forward(low, specs, [other[h]] * len(later), other_specs, rows, flux_parts))
        if w >= 0:
            here = [weighted[w], *low]
            if w + 1 < CHUNKS:
                done[:] = adjoint(here, [my_side(w, done[0]), their_side(w, done[1])], place, cells)
    (theirs,) = adjoint(here, [their_side(w, done[1])], place, cells)
    (mine,) = adjoint(here, [my_side(w, done[0])], place, cells)
    return paste(swapped(theirs), mine, place)[None]


def solution(mesh):
    devices = mesh.devices
    split = Mesh(devices.reshape(devices.shape[0], devices.shape[1] // 2, 2), ("tm", "z", "core"))
    cells = ("z", "core")
    placed = (P("tm", None, None, cells), P("tm", cells, None), P("tm", None), P("tm"))
    return jax.shard_map(
        on_device, mesh=split, in_specs=placed, out_specs=P("tm", cells, None), check_vma=False
    )
```
